32 devices in a mesh: groups: 2 (over y), users: 4 (over z), hours: 4 (over x, core).
Axes of the slice: x: 2, y: 2, z: 4, core: 2. Of those that a mesh axis runs over, the one named last changes fastest.
Arguments:
- activity: bfloat16 [16384, 8192], P(('groups', 'users'), 'hours'), parts along dimension 0, may hold values from -6 to 6
- cohort: int32 [16384], P(('groups', 'users')), parts along dimension 0, may hold values from 0 to 15
- tap_table: float32 [16, 9], replicated, may hold values from 0.02 to 0.4
- sketch: bfloat16 [8192, 64], P('hours'), may hold values from -0.0625 to 0.0625
Outputs:
- basis: float32 [16384, 64], P(('groups', 'users', 'hours')), parts along dimension 0
- triangle: float32 [128, 64], P('groups'), parts along dimension 0
The draws below stay inside these ranges and needn't reach their ends.
There are 2 independent parts, one for each index of `groups`. The reference program is written for one: setup_inputs(seed, part) draws one part's arguments, and reference() takes and returns one part's arrays. A program takes and returns all parts, laid end to end along the dimension named above; an argument that names none is the same for every part. Nothing has to cross between parts.
All inputs are finite; a program needn't handle non-finite values.
Results may differ from the reference program's by a relative error of at most 0.003.
Values may be sent and summed in bfloat16 or wider, within the bound.
A program may use at most 64 MiB of HBM per device.

```python
import jax
import jax.numpy as jnp
from jax import lax

K = 64
TAPS = 9
COHORTS = 16
U_DEV = 2048
U = 8192
H = 8192


def plant(drawn, key, low, largest):
    longest = drawn.shape.index(max(drawn.shape))
    spots = []
    for shift in (0, 1):
        where = [jax.random.randint(jax.random.fold_in(key, axis), (), 0, length) for axis, length in enumerate(drawn.shape)]
        where[longest] = (where[longest] + shift) % drawn.shape[longest]
        spots.append(tuple(where))
    return drawn.at[spots[0]].set(low).at[spots[1]].set(largest)


def block_scale(own_key, dims, shards, smallest, high):
    gain, own = 1.0, jax.random.fold_in(own_key, 6)
    for axis_at, parts in shards:
        heights = jnp.exp(jax.random.uniform(jax.random.fold_in(own, axis_at), (parts,), jnp.float32, smallest / len(shards), high / len(shards)))
        gain = gain * jnp.repeat(heights, dims[axis_at] // parts).reshape([-1 if axis == axis_at else 1 for axis in range(len(dims))])
    return gain


def scatter_about(stream_key, shape, width, limit, shards=(), kind=jnp.bfloat16):
    values = width * jax.random.normal(stream_key, shape, jnp.float32)
    if shards:
        values = values * block_scale(stream_key, shape, shards, -0.22, 0.18)
    return jnp.clip(values, -limit, limit).astype(kind)


def setup_inputs(seed: int = 0, part: int = 0) -> dict:
    key_list = jax.random.split(jax.random.key(seed), 5)
    part_splits = jax.random.split(jax.random.fold_in(key_list[4], part), 5)
    return {
        "activity": scatter_about(part_splits[0], (U, H), 1.0, 6.0, ((0, 4), (1, 4))),
        "cohort": plant(jax.random.randint(part_splits[1], (U,), 0, COHORTS), jax.random.fold_in(part_splits[1], 1), 0, COHORTS - 1).astype(jnp.int32),
        "tap_table": jnp.clip(jax.random.uniform(key_list[2], (COHORTS, TAPS), jnp.float32, 0.02, 0.4), 0.02, 0.4),
        "sketch": scatter_about(key_list[3], (H, K), H ** -0.5, 0.0625, ((0, 4),)),
    }


def smooth_block(rows_in, ids, tap_table, sketch):
    table_width = tap_table.shape[0]
    onehot = (ids[:, None] == jnp.arange(table_width, dtype=jnp.int32)[None, :]).astype(jnp.float32)
    taps = jnp.dot(onehot, tap_table, precision=lax.Precision.HIGHEST)
    reach = (TAPS - 1) // 2
    hours_all = rows_in.shape[1]
    padded = jnp.pad(rows_in, ((0, 0), (reach, reach)))
    total = jnp.zeros(rows_in.shape, jnp.float32)
    for step in range(TAPS):
        total = total + taps[:, step:step + 1] * padded[:, step:step + hours_all].astype(jnp.float32)
    smoothed = total.astype(jnp.bfloat16)
    return jnp.dot(smoothed.astype(jnp.float32), sketch.astype(jnp.float32), preferred_element_type=jnp.float32)

def reference(activity, cohort, tap_table, sketch):
    users_all, hours_all = activity.shape
    blocks = users_all // U_DEV
    stacked = activity.reshape(blocks, U_DEV, hours_all)
    ids = cohort.reshape(blocks, U_DEV)
    projected = lax.map(lambda pair: smooth_block(pair[0], pair[1], tap_table, sketch), (stacked, ids))
    projected = projected.reshape(users_all, sketch.shape[1])
    gram = jnp.dot(projected.T, projected, precision=lax.Precision.HIGHEST)
    lower = jnp.linalg.cholesky(gram)
    basis = lax.linalg.triangular_solve(lower, projected, left_side=False, lower=True, transpose_a=True)
    triangle = lower.T / jnp.sqrt(jnp.float32(users_all))
    return (basis, triangle)
```

```python
import functools
import math

import jax
import jax.numpy as jnp
from jax import lax
from jax.experimental import pallas as pl
from jax.experimental.pallas import tpu as pltpu
from jax.sharding import PartitionSpec as P

TAPS = 9
REACH = (TAPS - 1) // 2
EDGE = 128
SEAM = 2 * REACH
PICK = 16
PANEL = 8
HIGHEST = lax.Precision.HIGHEST
MESH = pl.DeviceIdType.MESH


def flip(index, mask):
    bit = 1
    while bit <= mask:
        if mask & bit:
            index = index + bit - 2 * bit * ((index // bit) % 2)
        bit *= 2
    return index


def dot_nt(a, b, precision=None):
    return lax.dot_general(
        a, b, (((1,), (1,)), ((), ())), precision=precision, preferred_element_type=jnp.float32
    )


def eliminate(gram):
    k = gram.shape[0]
    row_id = lax.broadcasted_iota(jnp.int32, (k, 2 * k), 0)
    lane_id = lax.broadcasted_iota(jnp.int32, (k, 2 * k), 1)
    eye = (row_id[:, :k] == lane_id[:, :k]).astype(jnp.float32)
    work = jnp.concatenate([gram, eye], axis=1)
    diag_id = lax.broadcasted_iota(jnp.int32, (PANEL, 2 * k), 0)
    done = []
    for first in range(0, k, PANEL):
        rows = work.shape[0]
        below = lax.broadcasted_iota(jnp.int32, (rows, 2 * k), 0)
        cols = [
            jnp.broadcast_to(work[:, first + i : first + i + 1], (rows, 2 * k))
            for i in range(PANEL)
        ]
        pivots = jnp.zeros((PANEL, 2 * k), jnp.float32)
        for i in range(PANEL):
            pivot = cols[i][i : i + 1, :]
            pivots = jnp.where(diag_id == i, pivot, pivots)
            col = jnp.where(below > i, cols[i], 0.0) * (1.0 / pivot)
            for later in range(i + 1, PANEL):
                cols[later] = cols[later] - col * cols[i][later : later + 1, :]
            work = work - col * work[i : i + 1, :]
        done.append(work[:PANEL] * lax.rsqrt(pivots))
        work = work[PANEL:]
    work = jnp.concatenate(done, axis=0)
    upper = jnp.where(row_id[:, :k] <= lane_id[:, :k], work[:, :k], 0.0)
    inverse = jnp.where(row_id[:, :k] >= lane_id[:, :k], work[:, k:], 0.0)
    return upper, inverse


def pack(square):
    half = square.shape[0] // 2
    return jnp.concatenate([square[:half], square[half:]], axis=1)


def unpack(packed):
    k = packed.shape[1] // 2
    return jnp.concatenate([packed[:, :k], packed[:, k:]], axis=0)


def combine(product, taps, k):
    total = taps[0:1, :] * product[:k]
    for step in range(1, TAPS):
        total += taps[step : step + 1, :] * product[step * k : (step + 1) * k]
    return total


def kernel(
    n_users, n_hours, activity, cohort_in, table_in, sketch_in, local_out, gram_out,
    block, cohort, table, sketch, shifted, taps, near_out, near_in, far_out, far_in,
    pick_out, picks, rims, gram_h, gram_u,
    load_sem, input_sem, near_send, near_recv, far_send, far_recv, pick_send, pick_recv,
    rim_send, rim_recv, gh_send, gh_recv, gu_send, gu_recv,
):
    users = lax.axis_index("users")
    hours = lax.axis_index("hours")
    rows, width = activity.shape
    k = sketch.shape[0]
    share = rows // n_hours
    half = share // 2

    order = list(range(n_hours - 1, 0, -1)) + [0]
    starts = [pl.multiple_of(flip(hours, mask) * share, share) for mask in range(n_hours)]
    inputs = [
        pltpu.make_async_copy(source, target, input_sem.at[i])
        for i, (source, target) in enumerate(
            ((sketch_in, sketch), (cohort_in, cohort), (table_in, table))
        )
    ]
    for copy in inputs:
        copy.start()
    loads = {}
    for mask in order:
        for part in range(2):
            load = pltpu.make_async_copy(
                activity.at[pl.ds(pl.multiple_of(starts[mask] + part * half, half), half), :],
                block.at[mask, pl.ds(part * half, half), :],
                load_sem.at[2 * mask + part],
            )
            load.start()
            loads[mask, part] = load

    barrier = pltpu.get_barrier_semaphore()
    for mask in range(1, n_hours):
        pl.semaphore_signal(
            barrier, inc=1, device_id={"hours": flip(hours, mask)}, device_id_type=MESH
        )
    for step in range(1, n_users):
        pl.semaphore_signal(
            barrier, inc=1, device_id={"users": (users + step) % n_users}, device_id_type=MESH
        )

    pick_row = lax.broadcasted_iota(jnp.int32, (PICK, width), 0)
    pick_lane = lax.broadcasted_iota(jnp.int32, (PICK, width), 1)
    wanted = jnp.where(pick_row < REACH, width - REACH + pick_row, pick_row - REACH)
    shifted[pl.ds(TAPS * k, PICK), :] = (
        (pick_lane == wanted) & (pick_row < SEAM)
    ).astype(jnp.bfloat16)

    inputs[0].wait()
    middle = sketch[...].astype(jnp.float32)
    lane = lax.broadcasted_iota(jnp.int32, (k, EDGE), 1)
    for step in range(TAPS):
        shift = step - REACH
        if shift == 0:
            shifted[pl.ds(step * k, k), :] = sketch[...]
            continue
        moved = pltpu.roll(middle, shift % width, 1)
        if shift > 0:
            first = jnp.where(lane < shift, 0.0, moved[:, :EDGE])
            moved = jnp.concatenate([first, moved[:, EDGE:]], axis=1)
        else:
            last = jnp.where(lane >= EDGE + shift, 0.0, moved[:, width - EDGE :])
            moved = jnp.concatenate([moved[:, : width - EDGE], last], axis=1)
        shifted[pl.ds(step * k, k), :] = moved.astype(jnp.bfloat16)

    inputs[1].wait()
    inputs[2].wait()
    cohorts = table.shape[0]
    onehot = (
        lax.broadcasted_iota(jnp.int32, (cohorts, rows), 0) == cohort[...]
    ).astype(jnp.float32)
    taps[...] = lax.dot_general(
        table[...], onehot, (((0,), (0,)), ((), ())),
        precision=HIGHEST, preferred_element_type=jnp.float32,
    )

    ends = jnp.where(
        lane < REACH,
        pltpu.roll(middle[:, width - EDGE :], REACH, 1),
        jnp.where(lane < SEAM, pltpu.roll(middle[:, :EDGE], REACH, 1), 0.0),
    )
    rims[hours] = ends

    waits = []

    def send(source, target, send_sem, recv_sem, mask):
        copy = pltpu.make_async_remote_copy(
            src_ref=source, dst_ref=target, send_sem=send_sem, recv_sem=recv_sem,
            device_id={"hours": flip(hours, mask)}, device_id_type=MESH,
        )
        copy.start()
        waits.append(copy)

    sums = {}
    for mask in order:
        for part in range(2):
            loads[mask, part].wait()
        product = jnp.concatenate(
            [
                dot_nt(shifted[...], block[mask, pl.ds(part * half, half), :])
                for part in range(2)
            ],
            axis=1,
        )
        total = combine(product, taps[:, pl.ds(starts[mask], share)], k)
        picked = product[TAPS * k : TAPS * k + SEAM]
        if mask == order[0]:
            pl.semaphore_wait(barrier, n_hours - 1 + n_users - 1)
            for other in range(1, n_hours):
                send(
                    rims.at[hours], rims.at[hours], rim_send.at[other - 1],
                    rim_recv.at[other - 1], other,
                )
        if mask == 0:
            picks[hours] = picked
            continue
        pick_out[mask - 1] = picked
        if mask == 1:
            near_out[...] = total
            send(near_out, near_in, near_send, near_recv, mask)
        else:
            far_out[mask - 2] = total.astype(jnp.bfloat16)
            send(
                far_out.at[mask - 2], far_in.at[mask - 2], far_send.at[mask - 2],
                far_recv.at[mask - 2], mask,
            )
        send(
            pick_out.at[mask - 1], picks.at[hours], pick_send.at[mask - 1],
            pick_recv.at[mask - 1], mask,
        )

    for copy in waits:
        copy.wait()

    seams = jnp.zeros((k, EDGE), jnp.float32)
    for index in range(n_hours - 1):
        left = jnp.where(lane < REACH, rims[index], 0.0)
        right = jnp.where(lane >= REACH, rims[index + 1], 0.0)
        both = left + right
        seams += both if index == 0 else pltpu.roll(both, SEAM * index, 1)
    row = lax.broadcasted_iota(jnp.int32, (SEAM, share), 0)
    beside = [
        jnp.where(row < REACH, picks[index], picks[index + 1]) for index in range(n_hours - 1)
    ]
    depth = EDGE // REACH
    beside = jnp.concatenate(
        beside + [jnp.zeros((depth - SEAM * (n_hours - 1), share), jnp.float32)], axis=0
    )
    place = lane % SEAM
    crossing, weighted = [], []
    for side in (-1, 1):
        panel = jnp.zeros((k, EDGE), jnp.float32)
        for index in range(REACH):
            shift = side * (index + 1)
            from_place = place - shift
            inside = (from_place >= 0) & (from_place < SEAM)
            across = (place < REACH) != (from_place < REACH)
            mine = (lane >= depth * index) & (lane < depth * (index + 1))
            moved = pltpu.roll(seams, (depth * index + shift) % EDGE, 1)
            panel = jnp.where(inside & across & mine, moved, panel)
            step = REACH + shift
            weighted.append(taps[pl.ds(step, 1), pl.ds(starts[0], share)] * beside)
        crossing.append(panel)
    total += jnp.dot(
        jnp.concatenate(crossing, axis=1).astype(jnp.bfloat16),
        jnp.concatenate(weighted, axis=0).astype(jnp.bfloat16),
        preferred_element_type=jnp.float32,
    )
    total += near_in[...]
    for mask in range(2, n_hours):
        total += far_in[mask - 2].astype(jnp.float32)
    local = total
    local_out[...] = local

    gram = pack(dot_nt(local, local, HIGHEST))
    for axis, count, me, slots, send_sems, recv_sems in (
        ("hours", n_hours, hours, gram_h, gh_send, gh_recv),
        ("users", n_users, users, gram_u, gu_send, gu_recv),
    ):
        slots[me] = gram
        copies = []
        for step in range(1, count):
            copy = pltpu.make_async_remote_copy(
                src_ref=slots.at[me],
                dst_ref=slots.at[me],
                send_sem=send_sems.at[step - 1],
                recv_sem=recv_sems.at[step - 1],
                device_id={axis: (me + step) % count},
                device_id_type=MESH,
            )
            copy.start()
            copies.append(copy)
        for copy in copies:
            copy.wait()
        gram = slots[0]
        for slot in range(1, count):
            gram = gram + slots[slot]

    gram_out[...] = gram


def finish(scale, local, gram, basis, triangle):
    upper, inverse = eliminate(unpack(gram[...]))
    triangle[...] = upper * scale
    high = inverse.astype(jnp.bfloat16)
    rest = (inverse - high.astype(jnp.float32)).astype(jnp.bfloat16)
    values = local[...]
    main = values.astype(jnp.bfloat16)
    minor = (values - main.astype(jnp.float32)).astype(jnp.bfloat16)
    basis[...] = jnp.dot(
        jnp.concatenate([high, rest, high], axis=1),
        jnp.concatenate([main, main, minor], axis=0),
        preferred_element_type=jnp.float32,
    )


def per_device(activity, cohort, tap_table, sketch):
    n_users, n_hours = lax.axis_size("users"), lax.axis_size("hours")
    rows, width = activity.shape
    k = sketch.shape[1]
    share = rows // n_hours
    dma = lambda count: pltpu.SemaphoreType.DMA((count,))
    one = pltpu.SemaphoreType.DMA
    vmem = pl.BlockSpec(memory_space=pltpu.VMEM)
    local, gram = pl.pallas_call(
        functools.partial(kernel, n_users, n_hours),
        out_shape=(
            pltpu.VMEM((k, share), jnp.float32),
            pltpu.VMEM((k // 2, 2 * k), jnp.float32),
        ),
        in_specs=[pl.BlockSpec(memory_space=pltpu.HBM)] * 4,
        out_specs=(vmem, vmem),
        scratch_shapes=[
            pltpu.VMEM((n_hours, share, width), jnp.bfloat16),
            pltpu.VMEM((1, rows), jnp.int32),
            pltpu.VMEM(tap_table.shape, jnp.float32),
            pltpu.VMEM((k, width), jnp.bfloat16),
            pltpu.VMEM((TAPS * k + PICK, width), jnp.bfloat16),
            pltpu.VMEM((TAPS, rows), jnp.float32),
            pltpu.VMEM((k, share), jnp.float32),
            pltpu.VMEM((k, share), jnp.float32),
            pltpu.VMEM((n_hours - 2, k, share), jnp.bfloat16),
            pltpu.VMEM((n_hours - 2, k, share), jnp.bfloat16),
            pltpu.VMEM((n_hours - 1, SEAM, share), jnp.float32),
            pltpu.VMEM((n_hours, SEAM, share), jnp.float32),
            pltpu.VMEM((n_hours, k, EDGE), jnp.float32),
            pltpu.VMEM((n_hours, k // 2, 2 * k), jnp.float32),
            pltpu.VMEM((n_users, k // 2, 2 * k), jnp.float32),
            dma(2 * n_hours), dma(3), one, one,
            dma(n_hours - 2), dma(n_hours - 2), dma(n_hours - 1), dma(n_hours - 1),
            dma(n_hours - 1), dma(n_hours - 1), dma(n_hours - 1), dma(n_hours - 1),
            dma(n_users - 1), dma(n_users - 1),
        ],
        compiler_params=pltpu.CompilerParams(
            collective_id=0, has_side_effects=True, vmem_limit_bytes=48 * 1024 * 1024
        ),
        name="range_finder",
    )(activity, cohort[None, :], tap_table, sketch.T)
    basis, triangle = pl.pallas_call(
        functools.partial(finish, 1.0 / math.sqrt(rows * n_users)),
        out_shape=(
            jax.ShapeDtypeStruct((k, share), jnp.float32),
            jax.ShapeDtypeStruct((k, k), jnp.float32),
        ),
        in_specs=[vmem, vmem],
        out_specs=(vmem, vmem),
        compiler_params=pltpu.CompilerParams(vmem_limit_bytes=8 * 1024 * 1024),
        name="factor",
    )(
        pltpu.with_memory_space_constraint(local, pltpu.VMEM),
        pltpu.with_memory_space_constraint(gram, pltpu.VMEM),
    )
    return basis.T, triangle


def solution(mesh):
    return jax.shard_map(
        per_device,
        mesh=mesh,
        in_specs=(P(("groups", "users"), "hours"), P(("groups", "users")), P(), P("hours", None)),
        out_specs=(P(("groups", "users", "hours"), None), P("groups", None)),
        check_vma=False,
    )
```

```python
import functools
import math

import jax
import jax.numpy as jnp
from jax import lax
from jax.experimental import pallas as pl
from jax.experimental.pallas import tpu as pltpu
from jax.sharding import PartitionSpec as P

TAPS = 9
REACH = (TAPS - 1) // 2
EDGE = 128
SEAM = 2 * REACH
PICK = 16
PANEL = 8
HIGHEST = lax.Precision.HIGHEST
MESH = pl.DeviceIdType.MESH


def flip(index, mask):
    bit = 1
    while bit <= mask:
        if mask & bit:
            index = index + bit - 2 * bit * ((index // bit) % 2)
        bit *= 2
    return index


def dot_nt(a, b, precision=None):
    return lax.dot_general(
        a, b, (((1,), (1,)), ((), ())), precision=precision, preferred_element_type=jnp.float32
    )


def eliminate(gram):
    k = gram.shape[0]
    row_id = lax.broadcasted_iota(jnp.int32, (k, 2 * k), 0)
    lane_id = lax.broadcasted_iota(jnp.int32, (k, 2 * k), 1)
    eye = (row_id[:, :k] == lane_id[:, :k]).astype(jnp.float32)
    work = jnp.concatenate([gram, eye], axis=1)
    diag_id = lax.broadcasted_iota(jnp.int32, (PANEL, 2 * k), 0)
    done = []
    for first in range(0, k, PANEL):
        rows = work.shape[0]
        below = lax.broadcasted_iota(jnp.int32, (rows, 2 * k), 0)
        cols = [
            jnp.broadcast_to(work[:, first + i : first + i + 1], (rows, 2 * k))
            for i in range(PANEL)
        ]
        pivots = jnp.zeros((PANEL, 2 * k), jnp.float32)
        for i in range(PANEL):
            pivot = cols[i][i : i + 1, :]
            pivots = jnp.where(diag_id == i, pivot, pivots)
            col = jnp.where(below > i, cols[i], 0.0) * (1.0 / pivot)
            for later in range(i + 1, PANEL):
                cols[later] = cols[later] - col * cols[i][later : later + 1, :]
            work = work - col * work[i : i + 1, :]
        done.append(work[:PANEL] * lax.rsqrt(pivots))
        work = work[PANEL:]
    work = jnp.concatenate(done, axis=0)
    upper = jnp.where(row_id[:, :k] <= lane_id[:, :k], work[:, :k], 0.0)
    inverse = jnp.where(row_id[:, :k] >= lane_id[:, :k], work[:, k:], 0.0)
    return upper, inverse


def pack(square):
    half = square.shape[0] // 2
    return jnp.concatenate([square[:half], square[half:]], axis=1)


def unpack(packed):
    k = packed.shape[1] // 2
    return jnp.concatenate([packed[:, :k], packed[:, k:]], axis=0)


def combine(product, taps, k):
    total = taps[0:1, :] * product[:k]
    for step in range(1, TAPS):
        total += taps[step : step + 1, :] * product[step * k : (step + 1) * k]
    return total


def kernel(
    n_users, n_hours, activity, cohort_in, table_in, sketch_in, local_out, gram_out,
    block, cohort, table, sketch, shifted, taps, near_out, near_in, far_out, far_in,
    pick_out, picks, rims, gram_h, gram_u,
    load_sem, input_sem, near_send, near_recv, far_send, far_recv, pick_send, pick_recv,
    rim_send, rim_recv, gh_send, gh_recv, gu_send, gu_recv,
):
    users = lax.axis_index("users")
    hours = lax.axis_index("hours")
    rows, width = activity.shape
    k = sketch.shape[0]
    share = rows // n_hours
    half = share // 2

    order = list(range(n_hours - 1, 0, -1)) + [0]
    starts = [pl.multiple_of(flip(hours, mask) * share, share) for mask in range(n_hours)]
    inputs = [
        pltpu.make_async_copy(source, target, input_sem.at[i])
        for i, (source, target) in enumerate(
            ((cohort_in, cohort), (table_in, table), (sketch_in, sketch))
        )
    ]
    for copy in inputs:
        copy.start()
    loads = {}
    for mask in order:
        for part in range(2):
            load = pltpu.make_async_copy(
                activity.at[pl.ds(pl.multiple_of(starts[mask] + part * half, half), half), :],
                block.at[mask, pl.ds(part * half, half), :],
                load_sem.at[2 * mask + part],
            )
            loads[mask, part] = load

    def fetch(index):
        if index < n_hours:
            for part in range(2):
                loads[order[index], part].start()

    fetch(0)

    barrier = pltpu.get_barrier_semaphore()
    for mask in range(1, n_hours):
        pl.semaphore_signal(
            barrier, inc=1, device_id={"hours": flip(hours, mask)}, device_id_type=MESH
        )
    for step in range(1, n_users):
        pl.semaphore_signal(
            barrier, inc=1, device_id={"users": (users + step) % n_users}, device_id_type=MESH
        )

    pick_row = lax.broadcasted_iota(jnp.int32, (PICK, width), 0)
    pick_lane = lax.broadcasted_iota(jnp.int32, (PICK, width), 1)
    wanted = jnp.where(pick_row < REACH, width - REACH + pick_row, pick_row - REACH)
    shifted[pl.ds(TAPS * k, PICK), :] = (
        (pick_lane == wanted) & (pick_row < SEAM)
    ).astype(jnp.bfloat16)

    inputs[0].wait()
    inputs[1].wait()
    cohorts = table.shape[0]
    onehot = (
        lax.broadcasted_iota(jnp.int32, (cohorts, rows), 0) == cohort[...]
    ).astype(jnp.float32)
    taps[...] = lax.dot_general(
        table[...], onehot, (((0,), (0,)), ((), ())),
        precision=HIGHEST, preferred_element_type=jnp.float32,
    )

    inputs[2].wait()
    fetch(1)
    middle = sketch[...].astype(jnp.float32)
    lane = lax.broadcasted_iota(jnp.int32, (k, EDGE), 1)
    for step in range(TAPS):
        shift = step - REACH
        if shift == 0:
            shifted[pl.ds(step * k, k), :] = sketch[...]
            continue
        moved = pltpu.roll(middle, shift % width, 1)
        if shift > 0:
            first = jnp.where(lane < shift, 0.0, moved[:, :EDGE])
            moved = jnp.concatenate([first, moved[:, EDGE:]], axis=1)
        else:
            last = jnp.where(lane >= EDGE + shift, 0.0, moved[:, width - EDGE :])
            moved = jnp.concatenate([moved[:, : width - EDGE], last], axis=1)
        shifted[pl.ds(step * k, k), :] = moved.astype(jnp.bfloat16)

    ends = jnp.where(
        lane < REACH,
        pltpu.roll(middle[:, width - EDGE :], REACH, 1),
        jnp.where(lane < SEAM, pltpu.roll(middle[:, :EDGE], REACH, 1), 0.0),
    )
    rims[hours] = ends

    waits = []

    def send(source, target, send_sem, recv_sem, mask):
        copy = pltpu.make_async_remote_copy(
            src_ref=source, dst_ref=target, send_sem=send_sem, recv_sem=recv_sem,
            device_id={"hours": flip(hours, mask)}, device_id_type=MESH,
        )
        copy.start()
        waits.append(copy)

    sums = {}
    for index, mask in enumerate(order):
        for part in range(2):
            loads[mask, part].wait()
        fetch(index + 2)
        product = jnp.concatenate(
            [
                dot_nt(shifted[...], block[mask, pl.ds(part * half, half), :])
                for part in range(2)
            ],
            axis=1,
        )
        total = combine(product, taps[:, pl.ds(starts[mask], share)], k)
        picked = product[TAPS * k : TAPS * k + SEAM]
        if mask == order[0]:
            pl.semaphore_wait(barrier, n_hours - 1 + n_users - 1)
            for other in range(1, n_hours):
                send(
                    rims.at[hours], rims.at[hours], rim_send.at[other - 1],
                    rim_recv.at[other - 1], other,
                )
        if mask == 0:
            picks[hours] = picked
            continue
        pick_out[mask - 1] = picked
        if mask == 1:
            near_out[...] = total
            send(near_out, near_in, near_send, near_recv, mask)
        else:
            far_out[mask - 2] = total.astype(jnp.bfloat16)
            send(
                far_out.at[mask - 2], far_in.at[mask - 2], far_send.at[mask - 2],
                far_recv.at[mask - 2], mask,
            )
        send(
            pick_out.at[mask - 1], picks.at[hours], pick_send.at[mask - 1],
            pick_recv.at[mask - 1], mask,
        )

    for copy in waits:
        copy.wait()

    seams = jnp.zeros((k, EDGE), jnp.float32)
    for index in range(n_hours - 1):
        left = jnp.where(lane < REACH, rims[index], 0.0)
        right = jnp.where(lane >= REACH, rims[index + 1], 0.0)
        both = left + right
        seams += both if index == 0 else pltpu.roll(both, SEAM * index, 1)
    row = lax.broadcasted_iota(jnp.int32, (SEAM, share), 0)
    beside = [
        jnp.where(row < REACH, picks[index], picks[index + 1]) for index in range(n_hours - 1)
    ]
    depth = EDGE // REACH
    beside = jnp.concatenate(
        beside + [jnp.zeros((depth - SEAM * (n_hours - 1), share), jnp.float32)], axis=0
    )
    place = lane % SEAM
    crossing, weighted = [], []
    for side in (-1, 1):
        panel = jnp.zeros((k, EDGE), jnp.float32)
        for index in range(REACH):
            shift = side * (index + 1)
            from_place = place - shift
            inside = (from_place >= 0) & (from_place < SEAM)
            across = (place < REACH) != (from_place < REACH)
            mine = (lane >= depth * index) & (lane < depth * (index + 1))
            moved = pltpu.roll(seams, (depth * index + shift) % EDGE, 1)
            panel = jnp.where(inside & across & mine, moved, panel)
            step = REACH + shift
            weighted.append(taps[pl.ds(step, 1), pl.ds(starts[0], share)] * beside)
        crossing.append(panel)
    total += jnp.dot(
        jnp.concatenate(crossing, axis=1).astype(jnp.bfloat16),
        jnp.concatenate(weighted, axis=0).astype(jnp.bfloat16),
        preferred_element_type=jnp.float32,
    )
    total += near_in[...]
    for mask in range(2, n_hours):
        total += far_in[mask - 2].astype(jnp.float32)
    local = total
    local_out[...] = local

    gram = pack(dot_nt(local, local, HIGHEST))
    for axis, count, me, slots, send_sems, recv_sems in (
        ("hours", n_hours, hours, gram_h, gh_send, gh_recv),
        ("users", n_users, users, gram_u, gu_send, gu_recv),
    ):
        slots[me] = gram
        copies = []
        for step in range(1, count):
            copy = pltpu.make_async_remote_copy(
                src_ref=slots.at[me],
                dst_ref=slots.at[me],
                send_sem=send_sems.at[step - 1],
                recv_sem=recv_sems.at[step - 1],
                device_id={axis: (me + step) % count},
                device_id_type=MESH,
            )
            copy.start()
            copies.append(copy)
        for copy in copies:
            copy.wait()
        gram = slots[0]
        for slot in range(1, count):
            gram = gram + slots[slot]

    gram_out[...] = gram


def finish(scale, local, gram, basis, triangle):
    upper, inverse = eliminate(unpack(gram[...]))
    triangle[...] = upper * scale
    high = inverse.astype(jnp.bfloat16)
    rest = (inverse - high.astype(jnp.float32)).astype(jnp.bfloat16)
    values = local[...]
    main = values.astype(jnp.bfloat16)
    minor = (values - main.astype(jnp.float32)).astype(jnp.bfloat16)
    basis[...] = jnp.dot(
        jnp.concatenate([high, rest, high], axis=1),
        jnp.concatenate([main, main, minor], axis=0),
        preferred_element_type=jnp.float32,
    )


def per_device(activity, cohort, tap_table, sketch):
    n_users, n_hours = lax.axis_size("users"), lax.axis_size("hours")
    rows, width = activity.shape
    k = sketch.shape[1]
    share = rows // n_hours
    dma = lambda count: pltpu.SemaphoreType.DMA((count,))
    one = pltpu.SemaphoreType.DMA
    vmem = pl.BlockSpec(memory_space=pltpu.VMEM)
    local, gram = pl.pallas_call(
        functools.partial(kernel, n_users, n_hours),
        out_shape=(
            pltpu.VMEM((k, share), jnp.float32),
            pltpu.VMEM((k // 2, 2 * k), jnp.float32),
        ),
        in_specs=[pl.BlockSpec(memory_space=pltpu.HBM)] * 4,
        out_specs=(vmem, vmem),
        scratch_shapes=[
            pltpu.VMEM((n_hours, share, width), jnp.bfloat16),
            pltpu.VMEM((1, rows), jnp.int32),
            pltpu.VMEM(tap_table.shape, jnp.float32),
            pltpu.VMEM((k, width), jnp.bfloat16),
            pltpu.VMEM((TAPS * k + PICK, width), jnp.bfloat16),
            pltpu.VMEM((TAPS, rows), jnp.float32),
            pltpu.VMEM((k, share), jnp.float32),
            pltpu.VMEM((k, share), jnp.float32),
            pltpu.VMEM((n_hours - 2, k, share), jnp.bfloat16),
            pltpu.VMEM((n_hours - 2, k, share), jnp.bfloat16),
            pltpu.VMEM((n_hours - 1, SEAM, share), jnp.float32),
            pltpu.VMEM((n_hours, SEAM, share), jnp.float32),
            pltpu.VMEM((n_hours, k, EDGE), jnp.float32),
            pltpu.VMEM((n_hours, k // 2, 2 * k), jnp.float32),
            pltpu.VMEM((n_users, k // 2, 2 * k), jnp.float32),
            dma(2 * n_hours), dma(3), one, one,
            dma(n_hours - 2), dma(n_hours - 2), dma(n_hours - 1), dma(n_hours - 1),
            dma(n_hours - 1), dma(n_hours - 1), dma(n_hours - 1), dma(n_hours - 1),
            dma(n_users - 1), dma(n_users - 1),
        ],
        compiler_params=pltpu.CompilerParams(
            collective_id=0, has_side_effects=True, vmem_limit_bytes=48 * 1024 * 1024
        ),
        name="range_finder",
    )(*(
        pltpu.with_memory_space_constraint(array, pltpu.HBM)
        for array in (activity, cohort[None, :], tap_table, sketch.T)
    ))
    basis, triangle = pl.pallas_call(
        functools.partial(finish, 1.0 / math.sqrt(rows * n_users)),
        out_shape=(
            jax.ShapeDtypeStruct((k, share), jnp.float32),
            jax.ShapeDtypeStruct((k, k), jnp.float32),
        ),
        in_specs=[vmem, vmem],
        out_specs=(vmem, vmem),
        compiler_params=pltpu.CompilerParams(vmem_limit_bytes=8 * 1024 * 1024),
        name="factor",
    )(
        pltpu.with_memory_space_constraint(local, pltpu.VMEM),
        pltpu.with_memory_space_constraint(gram, pltpu.VMEM),
    )
    return basis.T, triangle


def solution(mesh):
    return jax.shard_map(
        per_device,
        mesh=mesh,
        in_specs=(P(("groups", "users"), "hours"), P(("groups", "users")), P(), P("hours", None)),
        out_specs=(P(("groups", "users", "hours"), None), P("groups", None)),
        check_vma=False,
    )
```

```python
import functools
import math

import jax
import jax.numpy as jnp
from jax import lax
from jax.experimental import pallas as pl
from jax.experimental.pallas import tpu as pltpu
from jax.sharding import PartitionSpec as P

TAPS = 9
REACH = (TAPS - 1) // 2
EDGE = 128
SEAM = 2 * REACH
PICK = 16
PANEL = 8
HIGHEST = lax.Precision.HIGHEST
MESH = pl.DeviceIdType.MESH


def flip(index, mask):
    bit = 1
    while bit <= mask:
        if mask & bit:
            index = index + bit - 2 * bit * ((index // bit) % 2)
        bit *= 2
    return index


def dot_nt(a, b, precision=None):
    return lax.dot_general(
        a, b, (((1,), (1,)), ((), ())), precision=precision, preferred_element_type=jnp.float32
    )


def eliminate(gram):
    k = gram.shape[0]
    row_id = lax.broadcasted_iota(jnp.int32, (k, 2 * k), 0)
    lane_id = lax.broadcasted_iota(jnp.int32, (k, 2 * k), 1)
    eye = (row_id[:, :k] == lane_id[:, :k]).astype(jnp.float32)
    work = jnp.concatenate([gram, eye], axis=1)
    diag_id = lax.broadcasted_iota(jnp.int32, (PANEL, 2 * k), 0)
    done = []
    for first in range(0, k, PANEL):
        rows = work.shape[0]
        below = lax.broadcasted_iota(jnp.int32, (rows, 2 * k), 0)
        cols = [
            jnp.broadcast_to(work[:, first + i : first + i + 1], (rows, 2 * k))
            for i in range(PANEL)
        ]
        pivots = jnp.zeros((PANEL, 2 * k), jnp.float32)
        for i in range(PANEL):
            pivot = cols[i][i : i + 1, :]
            pivots = jnp.where(diag_id == i, pivot, pivots)
            col = jnp.where(below > i, cols[i], 0.0) * (1.0 / pivot)
            for later in range(i + 1, PANEL):
                cols[later] = cols[later] - col * cols[i][later : later + 1, :]
            work = work - col * work[i : i + 1, :]
        done.append(work[:PANEL] * lax.rsqrt(pivots))
        work = work[PANEL:]
    work = jnp.concatenate(done, axis=0)
    upper = jnp.where(row_id[:, :k] <= lane_id[:, :k], work[:, :k], 0.0)
    inverse = jnp.where(row_id[:, :k] >= lane_id[:, :k], work[:, k:], 0.0)
    return upper, inverse


def pack(square):
    k = square.shape[0]
    half = k // 2
    row = lax.broadcasted_iota(jnp.int32, (half, half), 0)
    col = lax.broadcasted_iota(jnp.int32, (half, half), 1)
    corner = square[half:, half:]
    folded = jnp.where(col >= row, square[:half, :half], corner)
    wide = jnp.concatenate([folded, square[:half, half:]], axis=1)
    diagonal = jnp.sum(jnp.where(row == col, corner, 0.0), axis=0, keepdims=True)
    diagonal = jnp.concatenate([diagonal, jnp.zeros((1, 2 * k - half), jnp.float32)], axis=1)
    quarter = half // 2
    return jnp.concatenate([wide[:quarter], wide[quarter:]], axis=1), diagonal


def unpack(packed):
    k = packed.shape[1] // 2
    half, quarter = k // 2, k // 4
    row = lax.broadcasted_iota(jnp.int32, (half, half), 0)
    col = lax.broadcasted_iota(jnp.int32, (half, half), 1)
    wide = jnp.concatenate([packed[:quarter, :k], packed[:quarter, k:]], axis=0)
    turned = wide.T
    upper, lower = wide[:, :half], turned[:half]
    corner = jnp.where(col < row, upper, lower)
    corner = jnp.where(col == row, packed[quarter : quarter + 1, :half], corner)
    first = jnp.where(col >= row, upper, lower)
    return jnp.concatenate(
        [
            jnp.concatenate([first, wide[:, half:]], axis=1),
            jnp.concatenate([turned[half:], corner], axis=1),
        ],
        axis=0,
    )


def combine(product, taps, k):
    total = taps[0:1, :] * product[:k]
    for step in range(1, TAPS):
        total += taps[step : step + 1, :] * product[step * k : (step + 1) * k]
    return total


def kernel(
    n_users, n_hours, activity, cohort_in, table_in, sketch_in, local_out, gram_out,
    block, cohort, table, sketch, shifted, taps, near_out, near_in, far_out, far_in,
    pick_out, picks, rims, grams,
    load_sem, input_sem, near_send, near_recv, far_send, far_recv, pick_send, pick_recv,
    rim_send, rim_recv, gram_send, gram_recv,
):
    users = lax.axis_index("users")
    hours = lax.axis_index("hours")
    rows, width = activity.shape
    k = sketch.shape[0]
    share = rows // n_hours
    half = share // 2

    order = list(range(n_hours - 1, 0, -1)) + [0]
    starts = [pl.multiple_of(flip(hours, mask) * share, share) for mask in range(n_hours)]
    inputs = [
        pltpu.make_async_copy(source, target, input_sem.at[i])
        for i, (source, target) in enumerate(
            ((cohort_in, cohort), (table_in, table), (sketch_in, sketch))
        )
    ]
    for copy in inputs:
        copy.start()
    loads = {}
    for mask in order:
        for part in range(2):
            load = pltpu.make_async_copy(
                activity.at[pl.ds(pl.multiple_of(starts[mask] + part * half, half), half), :],
                block.at[mask, pl.ds(part * half, half), :],
                load_sem.at[2 * mask + part],
            )
            loads[mask, part] = load

    def fetch(index):
        if index < n_hours:
            for part in range(2):
                loads[order[index], part].start()

    fetch(0)

    barrier = pltpu.get_barrier_semaphore()
    peers = [
        {"users": flip(users, far), "hours": flip(hours, mask)}
        for far in range(n_users - 1, -1, -1)
        for mask in range(n_hours - 1, -1, -1)
        if far or mask
    ]
    for peer in peers:
        pl.semaphore_signal(barrier, inc=1, device_id=peer, device_id_type=MESH)

    pick_row = lax.broadcasted_iota(jnp.int32, (PICK, width), 0)
    pick_lane = lax.broadcasted_iota(jnp.int32, (PICK, width), 1)
    wanted = jnp.where(pick_row < REACH, width - REACH + pick_row, pick_row - REACH)
    shifted[pl.ds(TAPS * k, PICK), :] = (
        (pick_lane == wanted) & (pick_row < SEAM)
    ).astype(jnp.bfloat16)

    inputs[0].wait()
    inputs[1].wait()
    cohorts = table.shape[0]
    onehot = (
        lax.broadcasted_iota(jnp.int32, (cohorts, rows), 0) == cohort[...]
    ).astype(jnp.float32)
    taps[...] = lax.dot_general(
        table[...], onehot, (((0,), (0,)), ((), ())),
        precision=HIGHEST, preferred_element_type=jnp.float32,
    )

    inputs[2].wait()
    fetch(1)
    middle = sketch[...].astype(jnp.float32)
    lane = lax.broadcasted_iota(jnp.int32, (k, EDGE), 1)
    for step in range(TAPS):
        shift = step - REACH
        if shift == 0:
            shifted[pl.ds(step * k, k), :] = sketch[...]
            continue
        moved = pltpu.roll(middle, shift % width, 1)
        if shift > 0:
            first = jnp.where(lane < shift, 0.0, moved[:, :EDGE])
            moved = jnp.concatenate([first, moved[:, EDGE:]], axis=1)
        else:
            last = jnp.where(lane >= EDGE + shift, 0.0, moved[:, width - EDGE :])
            moved = jnp.concatenate([moved[:, : width - EDGE], last], axis=1)
        shifted[pl.ds(step * k, k), :] = moved.astype(jnp.bfloat16)

    ends = jnp.where(
        lane < REACH,
        pltpu.roll(middle[:, width - EDGE :], REACH, 1),
        jnp.where(lane < SEAM, pltpu.roll(middle[:, :EDGE], REACH, 1), 0.0),
    )
    rims[hours] = ends

    small, late = [], []

    def send(source, target, send_sem, recv_sem, mask):
        copy = pltpu.make_async_remote_copy(
            src_ref=source, dst_ref=target, send_sem=send_sem, recv_sem=recv_sem,
            device_id={"hours": flip(hours, mask)}, device_id_type=MESH,
        )
        copy.start()
        return copy

    sums = {}
    for index, mask in enumerate(order):
        for part in range(2):
            loads[mask, part].wait()
        fetch(index + 2)
        product = jnp.concatenate(
            [
                dot_nt(shifted[...], block[mask, pl.ds(part * half, half), :])
                for part in range(2)
            ],
            axis=1,
        )
        total = combine(product, taps[:, pl.ds(starts[mask], share)], k)
        picked = product[TAPS * k : TAPS * k + SEAM]
        if mask == order[0]:
            pl.semaphore_wait(barrier, len(peers))
            for other in range(1, n_hours):
                small.append(send(
                    rims.at[hours], rims.at[hours], rim_send.at[other - 1],
                    rim_recv.at[other - 1], other,
                ))
        if mask == 0:
            picks[hours] = picked
            continue
        pick_out[mask - 1] = picked
        small.append(send(
            pick_out.at[mask - 1], picks.at[hours], pick_send.at[mask - 1],
            pick_recv.at[mask - 1], mask,
        ))
        if mask == 1:
            near_out[...] = total
            late.append(send(near_out, near_in, near_send, near_recv, mask))
        else:
            far_out[mask - 2] = total.astype(jnp.bfloat16)
            late.append(send(
                far_out.at[mask - 2], far_in.at[mask - 2], far_send.at[mask - 2],
                far_recv.at[mask - 2], mask,
            ))

    for copy in small:
        copy.wait()

    seams = jnp.zeros((k, EDGE), jnp.float32)
    for index in range(n_hours - 1):
        left = jnp.where(lane < REACH, rims[index], 0.0)
        right = jnp.where(lane >= REACH, rims[index + 1], 0.0)
        both = left + right
        seams += both if index == 0 else pltpu.roll(both, SEAM * index, 1)
    row = lax.broadcasted_iota(jnp.int32, (SEAM, share), 0)
    beside = [
        jnp.where(row < REACH, picks[index], picks[index + 1]) for index in range(n_hours - 1)
    ]
    depth = EDGE // REACH
    beside = jnp.concatenate(
        beside + [jnp.zeros((depth - SEAM * (n_hours - 1), share), jnp.float32)], axis=0
    )
    place = lane % SEAM
    crossing, weighted = [], []
    for side in (-1, 1):
        panel = jnp.zeros((k, EDGE), jnp.float32)
        for index in range(REACH):
            shift = side * (index + 1)
            from_place = place - shift
            inside = (from_place >= 0) & (from_place < SEAM)
            across = (place < REACH) != (from_place < REACH)
            mine = (lane >= depth * index) & (lane < depth * (index + 1))
            moved = pltpu.roll(seams, (depth * index + shift) % EDGE, 1)
            panel = jnp.where(inside & across & mine, moved, panel)
            step = REACH + shift
            weighted.append(taps[pl.ds(step, 1), pl.ds(starts[0], share)] * beside)
        crossing.append(panel)
    total += jnp.dot(
        jnp.concatenate(crossing, axis=1).astype(jnp.bfloat16),
        jnp.concatenate(weighted, axis=0).astype(jnp.bfloat16),
        preferred_element_type=jnp.float32,
    )
    for copy in reversed(late):
        copy.wait()
    total += near_in[...]
    for mask in range(2, n_hours):
        total += far_in[mask - 2].astype(jnp.float32)
    local = total
    local_out[...] = local

    me = users * n_hours + hours
    folded, diagonal = pack(dot_nt(local, local, HIGHEST))
    grams[me, pl.ds(0, k // 4), :] = folded
    grams[me, pl.ds(k // 4, 1), :] = diagonal
    copies = []
    for index, peer in enumerate(peers):
        copy = pltpu.make_async_remote_copy(
            src_ref=grams.at[me],
            dst_ref=grams.at[me],
            send_sem=gram_send.at[index],
            recv_sem=gram_recv.at[index],
            device_id=peer,
            device_id_type=MESH,
        )
        copy.start()
        copies.append(copy)
    for copy in copies:
        copy.wait_recv()
    gram = grams[0]
    for slot in range(1, n_users * n_hours):
        gram = gram + grams[slot]
    gram_out[...] = gram
    for copy in copies:
        copy.wait_send()


def finish(scale, local, gram, basis, triangle):
    upper, inverse = eliminate(unpack(gram[...]))
    triangle[...] = upper * scale
    high = inverse.astype(jnp.bfloat16)
    rest = (inverse - high.astype(jnp.float32)).astype(jnp.bfloat16)
    values = local[...]
    main = values.astype(jnp.bfloat16)
    minor = (values - main.astype(jnp.float32)).astype(jnp.bfloat16)
    basis[...] = jnp.dot(
        jnp.concatenate([high, rest, high], axis=1),
        jnp.concatenate([main, main, minor], axis=0),
        preferred_element_type=jnp.float32,
    )


def per_device(activity, cohort, tap_table, sketch):
    n_users, n_hours = lax.axis_size("users"), lax.axis_size("hours")
    rows, width = activity.shape
    k = sketch.shape[1]
    share = rows // n_hours
    dma = lambda count: pltpu.SemaphoreType.DMA((count,))
    one = pltpu.SemaphoreType.DMA
    vmem = pl.BlockSpec(memory_space=pltpu.VMEM)
    local, gram = pl.pallas_call(
        functools.partial(kernel, n_users, n_hours),
        out_shape=(
            pltpu.VMEM((k, share), jnp.float32),
            pltpu.VMEM((k // 4 + 1, 2 * k), jnp.float32),
        ),
        in_specs=[pl.BlockSpec(memory_space=pltpu.HBM)] * 4,
        out_specs=(vmem, vmem),
        scratch_shapes=[
            pltpu.VMEM((n_hours, share, width), jnp.bfloat16),
            pltpu.VMEM((1, rows), jnp.int32),
            pltpu.VMEM(tap_table.shape, jnp.float32),
            pltpu.VMEM((k, width), jnp.bfloat16),
            pltpu.VMEM((TAPS * k + PICK, width), jnp.bfloat16),
            pltpu.VMEM((TAPS, rows), jnp.float32),
            pltpu.VMEM((k, share), jnp.float32),
            pltpu.VMEM((k, share), jnp.float32),
            pltpu.VMEM((n_hours - 2, k, share), jnp.bfloat16),
            pltpu.VMEM((n_hours - 2, k, share), jnp.bfloat16),
            pltpu.VMEM((n_hours - 1, SEAM, share), jnp.float32),
            pltpu.VMEM((n_hours, SEAM, share), jnp.float32),
            pltpu.VMEM((n_hours, k, EDGE), jnp.float32),
            pltpu.VMEM((n_users * n_hours, k // 4 + 1, 2 * k), jnp.float32),
            dma(2 * n_hours), dma(3), one, one,
            dma(n_hours - 2), dma(n_hours - 2), dma(n_hours - 1), dma(n_hours - 1),
            dma(n_hours - 1), dma(n_hours - 1),
            dma(n_users * n_hours - 1), dma(n_users * n_hours - 1),
        ],
        compiler_params=pltpu.CompilerParams(
            collective_id=0, has_side_effects=True, vmem_limit_bytes=48 * 1024 * 1024
        ),
        name="range_finder",
    )(*(
        pltpu.with_memory_space_constraint(array, pltpu.HBM)
        for array in (activity, cohort[None, :], tap_table, sketch.T)
    ))
    basis, triangle = pl.pallas_call(
        functools.partial(finish, 1.0 / math.sqrt(rows * n_users)),
        out_shape=(
            jax.ShapeDtypeStruct((k, share), jnp.float32),
            jax.ShapeDtypeStruct((k, k), jnp.float32),
        ),
        in_specs=[vmem, vmem],
        out_specs=(vmem, vmem),
        compiler_params=pltpu.CompilerParams(vmem_limit_bytes=8 * 1024 * 1024),
        name="factor",
    )(
        pltpu.with_memory_space_constraint(local, pltpu.VMEM),
        pltpu.with_memory_space_constraint(gram, pltpu.VMEM),
    )
    return basis.T, triangle


def solution(mesh):
    return jax.shard_map(
        per_device,
        mesh=mesh,
        in_specs=(P(("groups", "users"), "hours"), P(("groups", "users")), P(), P("hours", None)),
        out_specs=(P(("groups", "users", "hours"), None), P("groups", None)),
        check_vma=False,
    )
```

```python
import functools
import math

import jax
import jax.numpy as jnp
from jax import lax
from jax.experimental import pallas as pl
from jax.experimental.pallas import tpu as pltpu
from jax.sharding import PartitionSpec as P

TAPS = 9
REACH = (TAPS - 1) // 2
EDGE = 128
SEAM = 2 * REACH
PICK = 16
PANEL = 16
HIGHEST = lax.Precision.HIGHEST
MESH = pl.DeviceIdType.MESH


def flip(index, mask):
    bit = 1
    while bit <= mask:
        if mask & bit:
            index = index + bit - 2 * bit * ((index // bit) % 2)
        bit *= 2
    return index


def dot_nt(a, b, precision=None):
    return lax.dot_general(
        a, b, (((1,), (1,)), ((), ())), precision=precision, preferred_element_type=jnp.float32
    )


def eliminate(gram):
    k = gram.shape[0]
    row_id = lax.broadcasted_iota(jnp.int32, (k, 2 * k), 0)
    lane_id = lax.broadcasted_iota(jnp.int32, (k, 2 * k), 1)
    eye = (row_id[:, :k] == lane_id[:, :k]).astype(jnp.float32)
    work = jnp.concatenate([gram, eye], axis=1)
    done = []
    for first in range(0, k, PANEL):
        rows = work.shape[0]
        below = lax.broadcasted_iota(jnp.int32, (rows, 2 * k), 0)
        cols = [
            jnp.broadcast_to(work[:, first + i : first + i + 1], (rows, 2 * k))
            for i in range(PANEL)
        ]
        for i in range(0, PANEL, 2):
            x, y = cols[i], cols[i + 1]
            a, b, d = x[i : i + 1, :], x[i + 1 : i + 2, :], y[i + 1 : i + 2, :]
            det = a * d - b * b
            inverse_det = 1.0 / det
            p = jnp.where(below > i + 1, d * x - b * y, 0.0) * inverse_det
            q = jnp.where(below > i + 1, a * y - b * x, 0.0) * inverse_det
            for later in range(i + 2, PANEL):
                cols[later] = cols[later] - (
                    p * x[later : later + 1, :] + q * y[later : later + 1, :]
                )
            top, second = work[i : i + 1, :], work[i + 1 : i + 2, :]
            work = work - (p * top + q * second)
            root = lax.rsqrt(a)
            done.append(top * root)
            done.append((second - (b * (1.0 / a)) * top) * (lax.rsqrt(det) * (a * root)))
        work = work[PANEL:]
    work = jnp.concatenate(done, axis=0)
    upper = jnp.where(row_id[:, :k] <= lane_id[:, :k], work[:, :k], 0.0)
    inverse = jnp.where(row_id[:, :k] >= lane_id[:, :k], work[:, k:], 0.0)
    return upper, inverse


def square(values):
    main = values.astype(jnp.bfloat16)
    minor = (values - main.astype(jnp.float32)).astype(jnp.bfloat16)
    both = dot_nt(main, minor)
    return dot_nt(main, main) + (both + both.T)


def pack(gram):
    k = gram.shape[0]
    half = k // 2
    row = lax.broadcasted_iota(jnp.int32, (half, half), 0)
    col = lax.broadcasted_iota(jnp.int32, (half, half), 1)
    corner = gram[half:, half:]
    folded = jnp.where(col >= row, gram[:half, :half], corner)
    wide = jnp.concatenate([folded, gram[:half, half:]], axis=1)
    diagonal = jnp.sum(jnp.where(row == col, corner, 0.0), axis=0, keepdims=True)
    diagonal = jnp.concatenate([diagonal, jnp.zeros((1, 2 * k - half), jnp.float32)], axis=1)
    quarter = half // 2
    return jnp.concatenate([wide[:quarter], wide[quarter:]], axis=1), diagonal


def unpack(packed):
    k = packed.shape[1] // 2
    half, quarter = k // 2, k // 4
    row = lax.broadcasted_iota(jnp.int32, (half, half), 0)
    col = lax.broadcasted_iota(jnp.int32, (half, half), 1)
    wide = jnp.concatenate([packed[:quarter, :k], packed[:quarter, k:]], axis=0)
    turned = wide.T
    upper, lower = wide[:, :half], turned[:half]
    corner = jnp.where(col < row, upper, lower)
    corner = jnp.where(col == row, packed[quarter : quarter + 1, :half], corner)
    first = jnp.where(col >= row, upper, lower)
    return jnp.concatenate(
        [
            jnp.concatenate([first, wide[:, half:]], axis=1),
            jnp.concatenate([turned[half:], corner], axis=1),
        ],
        axis=0,
    )


def combine(product, taps, k):
    total = taps[0:1, :] * product[:k]
    for step in range(1, TAPS):
        total += taps[step : step + 1, :] * product[step * k : (step + 1) * k]
    return total


def kernel(
    n_users, n_hours, activity, cohort_in, table_in, sketch_in, local_out, gram_out,
    block, cohort, table, sketch, shifted, taps, near_out, near_in, far_out, far_in,
    pick_out, picks, rims, grams,
    row_ready, load_sem, input_sem, part_send, part_recv, pick_send, pick_recv,
    rim_send, rim_recv, gram_send, gram_recv,
):
    users = lax.axis_index("users")
    hours = lax.axis_index("hours")
    rows, width = activity.shape
    k = sketch.shape[0]
    share = rows // n_hours
    half = share // 2

    order = list(range(n_hours - 1, 0, -1)) + [0]
    starts = [pl.multiple_of(flip(hours, mask) * share, share) for mask in range(n_hours)]
    inputs = [
        pltpu.make_async_copy(source, target, input_sem.at[i])
        for i, (source, target) in enumerate(
            ((cohort_in, cohort), (table_in, table), (sketch_in, sketch))
        )
    ]
    for copy in inputs:
        copy.start()
    loads = {}
    for mask in order:
        for part in range(2):
            load = pltpu.make_async_copy(
                activity.at[pl.ds(pl.multiple_of(starts[mask] + part * half, half), half), :],
                block.at[mask, pl.ds(part * half, half), :],
                load_sem.at[2 * mask + part],
            )
            loads[mask, part] = load

    def fetch(index):
        if index < n_hours:
            for part in range(2):
                loads[order[index], part].start()

    fetch(0)

    barrier = pltpu.get_barrier_semaphore()
    peers = [
        {"users": flip(users, far), "hours": flip(hours, mask)}
        for far in range(n_users - 1, -1, -1)
        for mask in range(n_hours - 1, -1, -1)
        if far or mask
    ]
    columns = [{"users": flip(users, far)} for far in range(n_users - 1, 0, -1)]
    for peer in [{"hours": flip(hours, mask)} for mask in range(n_hours - 1, 0, -1)] + columns:
        pl.semaphore_signal(barrier, inc=1, device_id=peer, device_id_type=MESH)

    pick_row = lax.broadcasted_iota(jnp.int32, (PICK, width), 0)
    pick_lane = lax.broadcasted_iota(jnp.int32, (PICK, width), 1)
    wanted = jnp.where(pick_row < REACH, width - REACH + pick_row, pick_row - REACH)
    shifted[pl.ds(TAPS * k, PICK), :] = (
        (pick_lane == wanted) & (pick_row < SEAM)
    ).astype(jnp.bfloat16)

    inputs[0].wait()
    inputs[1].wait()
    inputs[2].wait()
    fetch(1)
    middle = sketch[...].astype(jnp.float32)
    cohorts = table.shape[0]
    onehot = (
        lax.broadcasted_iota(jnp.int32, (cohorts, rows), 0) == cohort[...]
    ).astype(jnp.float32)
    taps[...] = lax.dot_general(
        table[...], onehot, (((0,), (0,)), ((), ())),
        precision=HIGHEST, preferred_element_type=jnp.float32,
    )

    lane = lax.broadcasted_iota(jnp.int32, (k, EDGE), 1)
    blank = jnp.zeros((k, EDGE), jnp.float32)
    padded = jnp.concatenate([blank, middle, blank], axis=1)
    for part in range(2):
        loads[order[0], part].wait()
    piece = width // 4
    products = [None, None]
    for first in range(0, width, piece):
        near_part = padded[:, first : first + piece + 2 * EDGE]
        for step in range(TAPS):
            shift = (step - REACH) % (piece + 2 * EDGE)
            moved = near_part if shift == 0 else pltpu.roll(near_part, shift, 1)
            shifted[pl.ds(step * k, k), pl.ds(first, piece)] = moved[
                :, EDGE : EDGE + piece
            ].astype(jnp.bfloat16)
        for part in range(2):
            partial = dot_nt(
                shifted[:, pl.ds(first, piece)],
                block[order[0], pl.ds(part * half, half), pl.ds(first, piece)],
            )
            products[part] = partial if first == 0 else products[part] + partial

    ends = jnp.where(
        lane < REACH,
        pltpu.roll(middle[:, width - EDGE :], REACH, 1),
        jnp.where(lane < SEAM, pltpu.roll(middle[:, :EDGE], REACH, 1), 0.0),
    )
    rims[hours] = jnp.concatenate(
        [ends.T[:SEAM], jnp.zeros((SEAM, EDGE - k), jnp.float32)], axis=1
    )

    small, copies = [], {}

    def send(source, target, send_sem, recv_sem, mask):
        copy = pltpu.make_async_remote_copy(
            src_ref=source, dst_ref=target, send_sem=send_sem, recv_sem=recv_sem,
            device_id={"hours": flip(hours, mask)}, device_id_type=MESH,
        )
        copy.start()
        return copy

    for index, mask in enumerate(order):
        if index:
            for part in range(2):
                loads[mask, part].wait()
        fetch(index + 2)
        sums, picked = [], []
        for part in range(2):
            if index:
                product = dot_nt(shifted[...], block[mask, pl.ds(part * half, half), :])
            else:
                product = products[part]
            start = pl.multiple_of(starts[mask] + part * half, half)
            sums.append(combine(product, taps[:, pl.ds(start, half)], k))
            picked.append(product[TAPS * k : TAPS * k + SEAM])
        total = jnp.concatenate(sums, axis=1)
        picked = jnp.concatenate(picked, axis=0).astype(jnp.bfloat16)
        if mask == order[0]:
            pl.semaphore_wait(barrier, n_hours + n_users - 2)
            for peer in columns:
                pl.semaphore_signal(row_ready, inc=1, device_id=peer, device_id_type=MESH)
            for other in range(1, n_hours):
                small.append(send(
                    rims.at[hours], rims.at[hours], rim_send.at[other - 1],
                    rim_recv.at[other - 1], other,
                ))
        if mask == 0:
            picks[hours] = picked
            continue
        bit = 1
        while mask + bit < n_hours and bit < mask & -mask:
            copies[mask + bit].wait()
            arrived = near_in if bit == 1 else far_in
            total += arrived[mask + bit - 1].astype(jnp.float32)
            bit *= 2
        near = mask % 2 == 1
        source, target = (near_out, near_in) if near else (far_out, far_in)
        source[mask - 1] = total.astype(source.dtype)
        copies[mask] = send(
            source.at[mask - 1], target.at[mask - 1], part_send.at[mask - 1],
            part_recv.at[mask - 1], mask & -mask,
        )
        pick_out[mask - 1] = picked
        small.append(send(
            pick_out.at[mask - 1], picks.at[hours], pick_send.at[mask - 1],
            pick_recv.at[mask - 1], mask,
        ))

    for copy in small:
        copy.wait()

    depth = EDGE // REACH
    rest = depth - SEAM * (n_hours - 1)

    def beside_seams(slots, count):
        row = lax.broadcasted_iota(jnp.int32, (SEAM, count), 0)
        return jnp.concatenate(
            [
                jnp.where(row < REACH, slots[index], slots[index + 1])
                for index in range(n_hours - 1)
            ]
            + [jnp.zeros((rest, count), jnp.float32)],
            axis=0,
        )

    seams = beside_seams([rims[index] for index in range(n_hours)], EDGE).T[:k]
    seams = jnp.concatenate([seams, jnp.zeros((k, EDGE - depth), jnp.float32)], axis=1)
    flat = [picks[index].astype(jnp.float32) for index in range(n_hours)]
    beside = beside_seams(
        [jnp.concatenate([pick[:SEAM], pick[SEAM:]], axis=1) for pick in flat], share
    )
    place = lane % SEAM
    crossing, weighted = [], []
    for side in (-1, 1):
        panel = jnp.zeros((k, EDGE), jnp.float32)
        for index in range(REACH):
            shift = side * (index + 1)
            from_place = place - shift
            inside = (from_place >= 0) & (from_place < SEAM)
            across = (place < REACH) != (from_place < REACH)
            mine = (lane >= depth * index) & (lane < depth * (index + 1))
            moved = pltpu.roll(seams, (depth * index + shift) % EDGE, 1)
            panel = jnp.where(inside & across & mine, moved, panel)
            step = REACH + shift
            weighted.append(taps[pl.ds(step, 1), pl.ds(starts[0], share)] * beside)
        crossing.append(panel)
    total += jnp.dot(
        jnp.concatenate(crossing, axis=1).astype(jnp.bfloat16),
        jnp.concatenate(weighted, axis=0).astype(jnp.bfloat16),
        preferred_element_type=jnp.float32,
    )
    bit = 1
    while bit < n_hours:
        copies[bit].wait()
        arrived = near_in if bit == 1 else far_in
        total += arrived[bit - 1].astype(jnp.float32)
        bit *= 2
    local = total
    local_out[...] = local

    me = users * n_hours + hours
    folded, diagonal = pack(square(local))
    grams[me, pl.ds(0, k // 4), :] = folded
    grams[me, pl.ds(k // 4, 1), :] = diagonal
    pl.semaphore_wait(row_ready, n_users - 1)
    copies = []
    for index, peer in enumerate(peers):
        copy = pltpu.make_async_remote_copy(
            src_ref=grams.at[me],
            dst_ref=grams.at[me],
            send_sem=gram_send.at[index],
            recv_sem=gram_recv.at[index],
            device_id=peer,
            device_id_type=MESH,
        )
        copy.start()
        copies.append(copy)
    for copy in copies:
        copy.wait_recv()
    gram = grams[0]
    for slot in range(1, n_users * n_hours):
        gram = gram + grams[slot]
    gram_out[...] = gram
    for copy in copies:
        copy.wait_send()


def finish(scale, local, gram, basis, triangle):
    upper, inverse = eliminate(unpack(gram[...]))
    triangle[...] = upper * scale
    high = inverse.astype(jnp.bfloat16)
    rest = (inverse - high.astype(jnp.float32)).astype(jnp.bfloat16)
    values = local[...]
    main = values.astype(jnp.bfloat16)
    minor = (values - main.astype(jnp.float32)).astype(jnp.bfloat16)
    basis[...] = jnp.dot(
        jnp.concatenate([high, rest, high], axis=1),
        jnp.concatenate([main, main, minor], axis=0),
        preferred_element_type=jnp.float32,
    )


def per_device(activity, cohort, tap_table, sketch):
    n_users, n_hours = lax.axis_size("users"), lax.axis_size("hours")
    rows, width = activity.shape
    k = sketch.shape[1]
    share = rows // n_hours
    dma = lambda count: pltpu.SemaphoreType.DMA((count,))
    vmem = pl.BlockSpec(memory_space=pltpu.VMEM)
    local, gram = pl.pallas_call(
        functools.partial(kernel, n_users, n_hours),
        out_shape=(
            pltpu.VMEM((k, share), jnp.float32),
            pltpu.VMEM((k // 4 + 1, 2 * k), jnp.float32),
        ),
        in_specs=[pl.BlockSpec(memory_space=pltpu.HBM)] * 4,
        out_specs=(vmem, vmem),
        scratch_shapes=[
            pltpu.VMEM((n_hours, share, width), jnp.bfloat16),
            pltpu.VMEM((1, rows), jnp.int32),
            pltpu.VMEM(tap_table.shape, jnp.float32),
            pltpu.VMEM((k, width), jnp.bfloat16),
            pltpu.VMEM((TAPS * k + PICK, width), jnp.bfloat16),
            pltpu.VMEM((TAPS, rows), jnp.float32),
            pltpu.VMEM((n_hours - 1, k, share), jnp.float32),
            pltpu.VMEM((n_hours - 1, k, share), jnp.float32),
            pltpu.VMEM((n_hours - 1, k, share), jnp.bfloat16),
            pltpu.VMEM((n_hours - 1, k, share), jnp.bfloat16),
            pltpu.VMEM((n_hours - 1, 2 * SEAM, share // 2), jnp.bfloat16),
            pltpu.VMEM((n_hours, 2 * SEAM, share // 2), jnp.bfloat16),
            pltpu.VMEM((n_hours, SEAM, EDGE), jnp.float32),
            pltpu.VMEM((n_users * n_hours, k // 4 + 1, 2 * k), jnp.float32),
            pltpu.SemaphoreType.REGULAR, dma(2 * n_hours), dma(3),
            dma(n_hours - 1), dma(n_hours - 1), dma(n_hours - 1), dma(n_hours - 1),
            dma(n_hours - 1), dma(n_hours - 1),
            dma(n_users * n_hours - 1), dma(n_users * n_hours - 1),
        ],
        compiler_params=pltpu.CompilerParams(
            collective_id=0, has_side_effects=True, vmem_limit_bytes=48 * 1024 * 1024
        ),
        name="range_finder",
    )(*(
        pltpu.with_memory_space_constraint(array, pltpu.HBM)
        for array in (activity, cohort[None, :], tap_table, sketch.T)
    ))
    basis, triangle = pl.pallas_call(
        functools.partial(finish, 1.0 / math.sqrt(rows * n_users)),
        out_shape=(
            jax.ShapeDtypeStruct((k, share), jnp.float32),
            jax.ShapeDtypeStruct((k, k), jnp.float32),
        ),
        in_specs=[vmem, vmem],
        out_specs=(vmem, vmem),
        compiler_params=pltpu.CompilerParams(vmem_limit_bytes=8 * 1024 * 1024),
        name="factor",
    )(
        pltpu.with_memory_space_constraint(local, pltpu.VMEM),
        pltpu.with_memory_space_constraint(gram, pltpu.VMEM),
    )
    return basis.T, triangle


def solution(mesh):
    return jax.shard_map(
        per_device,
        mesh=mesh,
        in_specs=(P(("groups", "users"), "hours"), P(("groups", "users")), P(), P("hours", None)),
        out_specs=(P(("groups", "users", "hours"), None), P("groups", None)),
        check_vma=False,
    )
```

```python
import functools
import math

import jax
import jax.numpy as jnp
from jax import lax
from jax.experimental import pallas as pl
from jax.experimental.pallas import tpu as pltpu
from jax.sharding import PartitionSpec as P

TAPS = 9
REACH = (TAPS - 1) // 2
EDGE = 128
SEAM = 2 * REACH
PICK = 16
PANEL = 16
HIGHEST = lax.Precision.HIGHEST
MESH = pl.DeviceIdType.MESH


def flip(index, mask):
    bit = 1
    while bit <= mask:
        if mask & bit:
            index = index + bit - 2 * bit * ((index // bit) % 2)
        bit *= 2
    return index


def dot_nt(a, b, precision=None):
    return lax.dot_general(
        a, b, (((1,), (1,)), ((), ())), precision=precision, preferred_element_type=jnp.float32
    )


def eliminate(gram):
    k = gram.shape[0]
    row_id = lax.broadcasted_iota(jnp.int32, (k, 2 * k), 0)
    lane_id = lax.broadcasted_iota(jnp.int32, (k, 2 * k), 1)
    eye = (row_id[:, :k] == lane_id[:, :k]).astype(jnp.float32)
    work = jnp.concatenate([gram, eye], axis=1)
    done = []
    for first in range(0, k, PANEL):
        rows = work.shape[0]
        below = lax.broadcasted_iota(jnp.int32, (rows, 2 * k), 0)
        cols = [
            jnp.broadcast_to(work[:, first + i : first + i + 1], (rows, 2 * k))
            for i in range(PANEL)
        ]
        for i in range(0, PANEL, 2):
            x, y = cols[i], cols[i + 1]
            a, b, d = x[i : i + 1, :], x[i + 1 : i + 2, :], y[i + 1 : i + 2, :]
            det = a * d - b * b
            inverse_det = 1.0 / det
            p = jnp.where(below > i + 1, d * x - b * y, 0.0) * inverse_det
            q = jnp.where(below > i + 1, a * y - b * x, 0.0) * inverse_det
            for later in range(i + 2, PANEL):
                cols[later] = cols[later] - (
                    p * x[later : later + 1, :] + q * y[later : later + 1, :]
                )
            top, second = work[i : i + 1, :], work[i + 1 : i + 2, :]
            work = work - (p * top + q * second)
            root = lax.rsqrt(a)
            done.append(top * root)
            done.append((second - (b * (1.0 / a)) * top) * (lax.rsqrt(det) * (a * root)))
        work = work[PANEL:]
    work = jnp.concatenate(done, axis=0)
    upper = jnp.where(row_id[:, :k] <= lane_id[:, :k], work[:, :k], 0.0)
    inverse = jnp.where(row_id[:, :k] >= lane_id[:, :k], work[:, k:], 0.0)
    return upper, inverse


def square(values):
    main = values.astype(jnp.bfloat16)
    minor = (values - main.astype(jnp.float32)).astype(jnp.bfloat16)
    return dot_nt(
        jnp.concatenate([main, main, minor], axis=1),
        jnp.concatenate([main, minor, main], axis=1),
    )


def pack(gram):
    k = gram.shape[0]
    half = k // 2
    row = lax.broadcasted_iota(jnp.int32, (half, half), 0)
    col = lax.broadcasted_iota(jnp.int32, (half, half), 1)
    corner = gram[half:, half:]
    folded = jnp.where(col >= row, gram[:half, :half], corner)
    wide = jnp.concatenate([folded, gram[:half, half:]], axis=1)
    diagonal = jnp.sum(jnp.where(row == col, corner, 0.0), axis=0, keepdims=True)
    diagonal = jnp.concatenate([diagonal, jnp.zeros((1, 2 * k - half), jnp.float32)], axis=1)
    quarter = half // 2
    return jnp.concatenate([wide[:quarter], wide[quarter:]], axis=1), diagonal


def unpack(packed):
    k = packed.shape[1] // 2
    half, quarter = k // 2, k // 4
    row = lax.broadcasted_iota(jnp.int32, (half, half), 0)
    col = lax.broadcasted_iota(jnp.int32, (half, half), 1)
    wide = jnp.concatenate([packed[:quarter, :k], packed[:quarter, k:]], axis=0)
    turned = wide.T
    upper, lower = wide[:, :half], turned[:half]
    corner = jnp.where(col < row, upper, lower)
    corner = jnp.where(col == row, packed[quarter : quarter + 1, :half], corner)
    first = jnp.where(col >= row, upper, lower)
    return jnp.concatenate(
        [
            jnp.concatenate([first, wide[:, half:]], axis=1),
            jnp.concatenate([turned[half:], corner], axis=1),
        ],
        axis=0,
    )


def combine(product, taps, k):
    total = taps[0:1, :] * product[:k]
    for step in range(1, TAPS):
        total += taps[step : step + 1, :] * product[step * k : (step + 1) * k]
    return total


def kernel(
    n_users, n_hours, activity, cohort_in, table_in, sketch_in, local_out, gram_out,
    block, cohort, table, sketch, shifted, taps, near_out, near_in, far_out, far_in,
    pick_out, picks, rims, grams,
    row_ready, load_sem, input_sem, part_send, part_recv, pick_send, pick_recv,
    rim_send, rim_recv, gram_send, gram_recv,
):
    users = lax.axis_index("users")
    hours = lax.axis_index("hours")
    rows, width = activity.shape
    k = sketch.shape[0]
    share = rows // n_hours
    half = share // 2

    order = list(range(n_hours - 1, 0, -1)) + [0]
    starts = [pl.multiple_of(flip(hours, mask) * share, share) for mask in range(n_hours)]
    inputs = [
        pltpu.make_async_copy(source, target, input_sem.at[i])
        for i, (source, target) in enumerate(
            ((cohort_in, cohort), (table_in, table), (sketch_in, sketch))
        )
    ]
    for copy in inputs:
        copy.start()
    loads = {}
    for mask in order:
        for part in range(2):
            load = pltpu.make_async_copy(
                activity.at[pl.ds(pl.multiple_of(starts[mask] + part * half, half), half), :],
                block.at[mask, pl.ds(part * half, half), :],
                load_sem.at[2 * mask + part],
            )
            loads[mask, part] = load

    def fetch(index):
        if index < n_hours:
            for part in range(2):
                loads[order[index], part].start()

    fetch(0)

    barrier = pltpu.get_barrier_semaphore()
    columns = [{"users": flip(users, far)} for far in range(n_users - 1, 0, -1)]
    for peer in [{"hours": flip(hours, mask)} for mask in range(n_hours - 1, 0, -1)] + columns:
        pl.semaphore_signal(barrier, inc=1, device_id=peer, device_id_type=MESH)

    pick_row = lax.broadcasted_iota(jnp.int32, (PICK, width), 0)
    pick_lane = lax.broadcasted_iota(jnp.int32, (PICK, width), 1)
    wanted = jnp.where(pick_row < REACH, width - REACH + pick_row, pick_row - REACH)
    shifted[pl.ds(TAPS * k, PICK), :] = (
        (pick_lane == wanted) & (pick_row < SEAM)
    ).astype(jnp.bfloat16)

    inputs[0].wait()
    inputs[1].wait()
    inputs[2].wait()
    fetch(1)
    middle = sketch[...].astype(jnp.float32)
    cohorts = table.shape[0]
    onehot = (
        lax.broadcasted_iota(jnp.int32, (cohorts, rows), 0) == cohort[...]
    ).astype(jnp.float32)
    taps[...] = lax.dot_general(
        table[...], onehot, (((0,), (0,)), ((), ())),
        precision=HIGHEST, preferred_element_type=jnp.float32,
    )

    lane = lax.broadcasted_iota(jnp.int32, (k, EDGE), 1)
    blank = jnp.zeros((k, EDGE), jnp.float32)
    padded = jnp.concatenate([blank, middle, blank], axis=1)
    for part in range(2):
        loads[order[0], part].wait()
    piece = width // 4
    products = [None, None]
    for first in range(0, width, piece):
        near_part = padded[:, first : first + piece + 2 * EDGE]
        for step in range(TAPS):
            shift = (step - REACH) % (piece + 2 * EDGE)
            moved = near_part if shift == 0 else pltpu.roll(near_part, shift, 1)
            shifted[pl.ds(step * k, k), pl.ds(first, piece)] = moved[
                :, EDGE : EDGE + piece
            ].astype(jnp.bfloat16)
        for part in range(2):
            partial = dot_nt(
                shifted[:, pl.ds(first, piece)],
                block[order[0], pl.ds(part * half, half), pl.ds(first, piece)],
            )
            products[part] = partial if first == 0 else products[part] + partial

    ends = jnp.where(
        lane < REACH,
        pltpu.roll(middle[:, width - EDGE :], REACH, 1),
        jnp.where(lane < SEAM, pltpu.roll(middle[:, :EDGE], REACH, 1), 0.0),
    )
    rims[hours] = jnp.concatenate(
        [ends.T[:SEAM], jnp.zeros((SEAM, EDGE - k), jnp.float32)], axis=1
    )

    small, copies = [], {}

    def send(source, target, send_sem, recv_sem, mask):
        copy = pltpu.make_async_remote_copy(
            src_ref=source, dst_ref=target, send_sem=send_sem, recv_sem=recv_sem,
            device_id={"hours": flip(hours, mask)}, device_id_type=MESH,
        )
        copy.start()
        return copy

    for index, mask in enumerate(order):
        if index:
            for part in range(2):
                loads[mask, part].wait()
        fetch(index + 2)
        sums, picked = [], []
        for part in range(2):
            if index:
                product = dot_nt(shifted[...], block[mask, pl.ds(part * half, half), :])
            else:
                product = products[part]
            start = pl.multiple_of(starts[mask] + part * half, half)
            sums.append(combine(product, taps[:, pl.ds(start, half)], k))
            picked.append(product[TAPS * k : TAPS * k + SEAM])
        total = jnp.concatenate(sums, axis=1)
        picked = jnp.concatenate(picked, axis=0).astype(jnp.bfloat16)
        if mask == order[0]:
            pl.semaphore_wait(barrier, n_hours + n_users - 2)
            for peer in columns:
                pl.semaphore_signal(row_ready, inc=1, device_id=peer, device_id_type=MESH)
            for other in range(1, n_hours):
                small.append(send(
                    rims.at[hours], rims.at[hours], rim_send.at[other - 1],
                    rim_recv.at[other - 1], other,
                ))
        if mask == 0:
            picks[hours] = picked
            continue
        bit = 1
        while mask + bit < n_hours and bit < mask & -mask:
            copies[mask + bit].wait()
            arrived = near_in if bit == 1 else far_in
            total += arrived[mask + bit - 1].astype(jnp.float32)
            bit *= 2
        near = mask % 2 == 1
        source, target = (near_out, near_in) if near else (far_out, far_in)
        source[mask - 1] = total.astype(source.dtype)
        copies[mask] = send(
            source.at[mask - 1], target.at[mask - 1], part_send.at[mask - 1],
            part_recv.at[mask - 1], mask & -mask,
        )
        pick_out[mask - 1] = picked
        small.append(send(
            pick_out.at[mask - 1], picks.at[hours], pick_send.at[mask - 1],
            pick_recv.at[mask - 1], mask,
        ))

    for copy in small:
        copy.wait()

    depth = EDGE // REACH
    rest = depth - SEAM * (n_hours - 1)

    def beside_seams(slots, count):
        row = lax.broadcasted_iota(jnp.int32, (SEAM, count), 0)
        return jnp.concatenate(
            [
                jnp.where(row < REACH, slots[index], slots[index + 1])
                for index in range(n_hours - 1)
            ]
            + [jnp.zeros((rest, count), jnp.float32)],
            axis=0,
        )

    seams = beside_seams([rims[index] for index in range(n_hours)], EDGE).T[:k]
    seams = jnp.concatenate([seams, jnp.zeros((k, EDGE - depth), jnp.float32)], axis=1)
    flat = [picks[index].astype(jnp.float32) for index in range(n_hours)]
    beside = beside_seams(
        [jnp.concatenate([pick[:SEAM], pick[SEAM:]], axis=1) for pick in flat], share
    )
    place = lane % SEAM
    crossing, weighted = [], []
    for side in (-1, 1):
        panel = jnp.zeros((k, EDGE), jnp.float32)
        for index in range(REACH):
            shift = side * (index + 1)
            from_place = place - shift
            inside = (from_place >= 0) & (from_place < SEAM)
            across = (place < REACH) != (from_place < REACH)
            mine = (lane >= depth * index) & (lane < depth * (index + 1))
            moved = pltpu.roll(seams, (depth * index + shift) % EDGE, 1)
            panel = jnp.where(inside & across & mine, moved, panel)
            step = REACH + shift
            weighted.append(taps[pl.ds(step, 1), pl.ds(starts[0], share)] * beside)
        crossing.append(panel)
    total += jnp.dot(
        jnp.concatenate(crossing, axis=1).astype(jnp.bfloat16),
        jnp.concatenate(weighted, axis=0).astype(jnp.bfloat16),
        preferred_element_type=jnp.float32,
    )
    bit = 1
    while bit < n_hours:
        copies[bit].wait()
        arrived = near_in if bit == 1 else far_in
        total += arrived[bit - 1].astype(jnp.float32)
        bit *= 2
    local = total
    local_out[...] = local

    me = users * n_hours + hours
    folded, diagonal = pack(square(local))
    grams[me, pl.ds(0, k // 4), :] = folded
    grams[me, pl.ds(k // 4, 1), :] = diagonal
    pl.semaphore_wait(row_ready, n_users - 1)
    upper_half = users // (n_users // 2)
    outgoing, incoming = [], []
    for index in range(n_users):
        down = n_users - 2 - index
        down += (down - users + n_users) // n_users
        up = index + (index - users + n_users) // n_users
        target = upper_half * up + (1 - upper_half) * down if index < n_users - 1 else users
        for mask in range(n_hours - 1, -1, -1):
            if index == n_users - 1 and mask == 0:
                continue
            beside = flip(hours, mask)
            slot = target * n_hours + beside
            copy = pltpu.make_async_remote_copy(
                src_ref=grams.at[me],
                dst_ref=grams.at[me],
                send_sem=gram_send.at[slot],
                recv_sem=gram_recv.at[me],
                device_id={"users": target, "hours": beside},
                device_id_type=MESH,
            )
            copy.start()
            outgoing.append(copy)
            incoming.append(
                pltpu.make_async_remote_copy(
                    src_ref=grams.at[slot],
                    dst_ref=grams.at[slot],
                    send_sem=gram_send.at[slot],
                    recv_sem=gram_recv.at[slot],
                    device_id={"users": target, "hours": beside},
                    device_id_type=MESH,
                )
            )
    for copy in incoming:
        copy.wait_recv()
    gram = grams[0]
    for slot in range(1, n_users * n_hours):
        gram = gram + grams[slot]
    gram_out[...] = gram
    for copy in outgoing:
        copy.wait_send()


def finish(scale, local, gram, basis, triangle):
    upper, inverse = eliminate(unpack(gram[...]))
    triangle[...] = upper * scale
    high = inverse.astype(jnp.bfloat16)
    rest = (inverse - high.astype(jnp.float32)).astype(jnp.bfloat16)
    values = local[...]
    main = values.astype(jnp.bfloat16)
    minor = (values - main.astype(jnp.float32)).astype(jnp.bfloat16)
    basis[...] = jnp.dot(
        jnp.concatenate([high, rest, high], axis=1),
        jnp.concatenate([main, main, minor], axis=0),
        preferred_element_type=jnp.float32,
    )


def per_device(activity, cohort, tap_table, sketch):
    n_users, n_hours = lax.axis_size("users"), lax.axis_size("hours")
    rows, width = activity.shape
    k = sketch.shape[1]
    share = rows // n_hours
    dma = lambda count: pltpu.SemaphoreType.DMA((count,))
    vmem = pl.BlockSpec(memory_space=pltpu.VMEM)
    local, gram = pl.pallas_call(
        functools.partial(kernel, n_users, n_hours),
        out_shape=(
            pltpu.VMEM((k, share), jnp.float32),
            pltpu.VMEM((k // 4 + 1, 2 * k), jnp.float32),
        ),
        in_specs=[pl.BlockSpec(memory_space=pltpu.HBM)] * 4,
        out_specs=(vmem, vmem),
        scratch_shapes=[
            pltpu.VMEM((n_hours, share, width), jnp.bfloat16),
            pltpu.VMEM((1, rows), jnp.int32),
            pltpu.VMEM(tap_table.shape, jnp.float32),
            pltpu.VMEM((k, width), jnp.bfloat16),
            pltpu.VMEM((TAPS * k + PICK, width), jnp.bfloat16),
            pltpu.VMEM((TAPS, rows), jnp.float32),
            pltpu.VMEM((n_hours - 1, k, share), jnp.float32),
            pltpu.VMEM((n_hours - 1, k, share), jnp.float32),
            pltpu.VMEM((n_hours - 1, k, share), jnp.bfloat16),
            pltpu.VMEM((n_hours - 1, k, share), jnp.bfloat16),
            pltpu.VMEM((n_hours - 1, 2 * SEAM, share // 2), jnp.bfloat16),
            pltpu.VMEM((n_hours, 2 * SEAM, share // 2), jnp.bfloat16),
            pltpu.VMEM((n_hours, SEAM, EDGE), jnp.float32),
            pltpu.VMEM((n_users * n_hours, k // 4 + 1, 2 * k), jnp.float32),
            pltpu.SemaphoreType.REGULAR, dma(2 * n_hours), dma(3),
            dma(n_hours - 1), dma(n_hours - 1), dma(n_hours - 1), dma(n_hours - 1),
            dma(n_hours - 1), dma(n_hours - 1),
            dma(n_users * n_hours), dma(n_users * n_hours),
        ],
        compiler_params=pltpu.CompilerParams(
            collective_id=0, has_side_effects=True, vmem_limit_bytes=48 * 1024 * 1024
        ),
        name="range_finder",
    )(*(
        pltpu.with_memory_space_constraint(array, pltpu.HBM)
        for array in (activity, cohort[None, :], tap_table, sketch.T)
    ))
    basis, triangle = pl.pallas_call(
        functools.partial(finish, 1.0 / math.sqrt(rows * n_users)),
        out_shape=(
            jax.ShapeDtypeStruct((k, share), jnp.float32),
            jax.ShapeDtypeStruct((k, k), jnp.float32),
        ),
        in_specs=[vmem, vmem],
        out_specs=(vmem, vmem),
        compiler_params=pltpu.CompilerParams(vmem_limit_bytes=8 * 1024 * 1024),
        name="factor",
    )(
        pltpu.with_memory_space_constraint(local, pltpu.VMEM),
        pltpu.with_memory_space_constraint(gram, pltpu.VMEM),
    )
    return basis.T, triangle


def solution(mesh):
    return jax.shard_map(
        per_device,
        mesh=mesh,
        in_specs=(P(("groups", "users"), "hours"), P(("groups", "users")), P(), P("hours", None)),
        out_specs=(P(("groups", "users", "hours"), None), P("groups", None)),
        check_vma=False,
    )
```

```python
import functools
import math

import jax
import jax.numpy as jnp
from jax import lax
from jax.experimental import pallas as pl
from jax.experimental.pallas import tpu as pltpu
from jax.sharding import PartitionSpec as P

TAPS = 9
REACH = (TAPS - 1) // 2
EDGE = 128
SEAM = 2 * REACH
PICK = 16
PANEL = 16
HIGHEST = lax.Precision.HIGHEST
MESH = pl.DeviceIdType.MESH


def flip(index, mask):
    bit = 1
    while bit <= mask:
        if mask & bit:
            index = index + bit - 2 * bit * ((index // bit) % 2)
        bit *= 2
    return index


def dot_nt(a, b, precision=None):
    return lax.dot_general(
        a, b, (((1,), (1,)), ((), ())), precision=precision, preferred_element_type=jnp.float32
    )


def eliminate(gram):
    k = gram.shape[0]
    row_id = lax.broadcasted_iota(jnp.int32, (k, 2 * k), 0)
    lane_id = lax.broadcasted_iota(jnp.int32, (k, 2 * k), 1)
    eye = (row_id[:, :k] == lane_id[:, :k]).astype(jnp.float32)
    work = jnp.concatenate([gram, eye], axis=1)
    done = []
    for first in range(0, k, PANEL):
        rows = work.shape[0]
        below = lax.broadcasted_iota(jnp.int32, (rows, 2 * k), 0)
        cols = [
            jnp.broadcast_to(work[:, first + i : first + i + 1], (rows, 2 * k))
            for i in range(PANEL)
        ]
        for i in range(0, PANEL, 2):
            x, y = cols[i], cols[i + 1]
            a, b, d = x[i : i + 1, :], x[i + 1 : i + 2, :], y[i + 1 : i + 2, :]
            det = a * d - b * b
            inverse_det = 1.0 / det
            p = jnp.where(below > i + 1, d * x - b * y, 0.0) * inverse_det
            q = jnp.where(below > i + 1, a * y - b * x, 0.0) * inverse_det
            for later in range(i + 2, PANEL):
                cols[later] = cols[later] - (
                    p * x[later : later + 1, :] + q * y[later : later + 1, :]
                )
            top, second = work[i : i + 1, :], work[i + 1 : i + 2, :]
            work = work - (p * top + q * second)
            root = lax.rsqrt(a)
            done.append(top * root)
            done.append((second - (b * (1.0 / a)) * top) * (lax.rsqrt(det) * (a * root)))
        work = work[PANEL:]
    work = jnp.concatenate(done, axis=0)
    upper = jnp.where(row_id[:, :k] <= lane_id[:, :k], work[:, :k], 0.0)
    inverse = jnp.where(row_id[:, :k] >= lane_id[:, :k], work[:, k:], 0.0)
    return upper, inverse


def square(values):
    main = values.astype(jnp.bfloat16)
    minor = (values - main.astype(jnp.float32)).astype(jnp.bfloat16)
    return dot_nt(
        jnp.concatenate([main, main, minor], axis=1),
        jnp.concatenate([main, minor, main], axis=1),
    )


def pack(gram):
    k = gram.shape[0]
    half = k // 2
    row = lax.broadcasted_iota(jnp.int32, (half, half), 0)
    col = lax.broadcasted_iota(jnp.int32, (half, half), 1)
    corner = gram[half:, half:]
    folded = jnp.where(col >= row, gram[:half, :half], corner)
    wide = jnp.concatenate([folded, gram[:half, half:]], axis=1)
    diagonal = jnp.sum(jnp.where(row == col, corner, 0.0), axis=0, keepdims=True)
    diagonal = jnp.concatenate([diagonal, jnp.zeros((1, 2 * k - half), jnp.float32)], axis=1)
    quarter = half // 2
    return jnp.concatenate([wide[:quarter], wide[quarter:]], axis=1), diagonal


def unpack(packed):
    k = packed.shape[1] // 2
    half, quarter = k // 2, k // 4
    row = lax.broadcasted_iota(jnp.int32, (half, half), 0)
    col = lax.broadcasted_iota(jnp.int32, (half, half), 1)
    wide = jnp.concatenate([packed[:quarter, :k], packed[:quarter, k:]], axis=0)
    turned = wide.T
    upper, lower = wide[:, :half], turned[:half]
    corner = jnp.where(col < row, upper, lower)
    corner = jnp.where(col == row, packed[quarter : quarter + 1, :half], corner)
    first = jnp.where(col >= row, upper, lower)
    return jnp.concatenate(
        [
            jnp.concatenate([first, wide[:, half:]], axis=1),
            jnp.concatenate([turned[half:], corner], axis=1),
        ],
        axis=0,
    )


def combine(product, taps, k):
    total = taps[0:1, :] * product[:k]
    for step in range(1, TAPS):
        total += taps[step : step + 1, :] * product[step * k : (step + 1) * k]
    return total


def kernel(
    n_users, n_hours, activity, cohort_in, table_in, sketch_in, local_out, gram_out,
    block, cohort, table, sketch, shifted, taps, near_out, near_in, far_out, far_in,
    pick_out, picks, rims, grams,
    row_ready, load_sem, input_sem, part_send, part_recv, pick_send, pick_recv,
    rim_send, rim_recv, gram_send, gram_recv,
):
    users = lax.axis_index("users")
    hours = lax.axis_index("hours")
    rows, width = activity.shape
    k = sketch.shape[0]
    share = rows // n_hours
    half = share // 2

    order = list(range(n_hours - 1, 0, -1)) + [0]
    starts = [pl.multiple_of(flip(hours, mask) * share, share) for mask in range(n_hours)]
    inputs = [
        pltpu.make_async_copy(source, target, input_sem.at[i])
        for i, (source, target) in enumerate(
            ((cohort_in, cohort), (table_in, table), (sketch_in, sketch))
        )
    ]
    for copy in inputs:
        copy.start()
    loads = {}
    for mask in order:
        for part in range(2):
            load = pltpu.make_async_copy(
                activity.at[pl.ds(pl.multiple_of(starts[mask] + part * half, half), half), :],
                block.at[mask, pl.ds(part * half, half), :],
                load_sem.at[2 * mask + part],
            )
            loads[mask, part] = load

    def fetch(index):
        if index < n_hours:
            for part in range(2):
                loads[order[index], part].start()

    fetch(0)

    barrier = pltpu.get_barrier_semaphore()
    columns = [{"users": flip(users, far)} for far in range(n_users - 1, 0, -1)]
    for peer in [{"hours": flip(hours, mask)} for mask in range(n_hours - 1, 0, -1)] + columns:
        pl.semaphore_signal(barrier, inc=1, device_id=peer, device_id_type=MESH)

    pick_row = lax.broadcasted_iota(jnp.int32, (PICK, width), 0)
    pick_lane = lax.broadcasted_iota(jnp.int32, (PICK, width), 1)
    wanted = jnp.where(pick_row < REACH, width - REACH + pick_row, pick_row - REACH)
    shifted[pl.ds(TAPS * k, PICK), :] = (
        (pick_lane == wanted) & (pick_row < SEAM)
    ).astype(jnp.bfloat16)

    inputs[0].wait()
    inputs[1].wait()
    inputs[2].wait()
    fetch(1)
    middle = sketch[...].astype(jnp.float32)
    cohorts = table.shape[0]
    onehot = (
        lax.broadcasted_iota(jnp.int32, (cohorts, rows), 0) == cohort[...]
    ).astype(jnp.float32)
    taps[...] = lax.dot_general(
        table[...], onehot, (((0,), (0,)), ((), ())),
        precision=HIGHEST, preferred_element_type=jnp.float32,
    )

    lane = lax.broadcasted_iota(jnp.int32, (k, EDGE), 1)
    blank = jnp.zeros((k, EDGE), jnp.float32)
    padded = jnp.concatenate([blank, middle, blank], axis=1)
    for part in range(2):
        loads[order[0], part].wait()
    piece = width // 4
    products = [None, None]
    for first in range(0, width, piece):
        near_part = padded[:, first : first + piece + 2 * EDGE]
        for step in range(TAPS):
            shift = (step - REACH) % (piece + 2 * EDGE)
            moved = near_part if shift == 0 else pltpu.roll(near_part, shift, 1)
            shifted[pl.ds(step * k, k), pl.ds(first, piece)] = moved[
                :, EDGE : EDGE + piece
            ].astype(jnp.bfloat16)
        for part in range(2):
            partial = dot_nt(
                shifted[:, pl.ds(first, piece)],
                block[order[0], pl.ds(part * half, half), pl.ds(first, piece)],
            )
            products[part] = partial if first == 0 else products[part] + partial

    ends = jnp.where(
        lane < REACH,
        pltpu.roll(middle[:, width - EDGE :], REACH, 1),
        jnp.where(lane < SEAM, pltpu.roll(middle[:, :EDGE], REACH, 1), 0.0),
    )
    rims[hours] = jnp.concatenate(
        [ends.T[:SEAM], jnp.zeros((SEAM, EDGE - k), jnp.float32)], axis=1
    )

    small, copies = [], {}

    def send(source, target, send_sem, recv_sem, mask):
        copy = pltpu.make_async_remote_copy(
            src_ref=source, dst_ref=target, send_sem=send_sem, recv_sem=recv_sem,
            device_id={"hours": flip(hours, mask)}, device_id_type=MESH,
        )
        copy.start()
        return copy

    for index, mask in enumerate(order):
        if index:
            for part in range(2):
                loads[mask, part].wait()
        fetch(index + 2)
        sums, picked = [], []
        for part in range(2):
            if index:
                product = dot_nt(shifted[...], block[mask, pl.ds(part * half, half), :])
            else:
                product = products[part]
            start = pl.multiple_of(starts[mask] + part * half, half)
            sums.append(combine(product, taps[:, pl.ds(start, half)], k))
            picked.append(product[TAPS * k : TAPS * k + SEAM])
        total = jnp.concatenate(sums, axis=1)
        picked = jnp.concatenate(picked, axis=0).astype(jnp.bfloat16)
        if mask == order[0]:
            pl.semaphore_wait(barrier, n_hours + n_users - 2)
        if mask == 0:
            picks[hours] = picked
            continue
        bit = 1
        while mask + bit < n_hours and bit < mask & -mask:
            copies[mask + bit].wait_recv()
            arrived = near_in if bit == 1 else far_in
            total += arrived[mask + bit - 1].astype(jnp.float32)
            bit *= 2
        near = mask % 2 == 1
        source, target = (near_out, near_in) if near else (far_out, far_in)
        source[mask - 1] = total.astype(source.dtype)
        copies[mask] = send(
            source.at[mask - 1], target.at[mask - 1], part_send.at[mask - 1],
            part_recv.at[mask - 1], mask & -mask,
        )
        if mask == order[0]:
            for peer in columns:
                pl.semaphore_signal(row_ready, inc=1, device_id=peer, device_id_type=MESH)
            for other in range(1, n_hours):
                small.append(send(
                    rims.at[hours], rims.at[hours], rim_send.at[other - 1],
                    rim_recv.at[other - 1], other,
                ))
        pick_out[mask - 1] = picked
        small.append(send(
            pick_out.at[mask - 1], picks.at[hours], pick_send.at[mask - 1],
            pick_recv.at[mask - 1], mask,
        ))

    for copy in small:
        copy.wait_recv()

    depth = EDGE // REACH
    rest = depth - SEAM * (n_hours - 1)

    def beside_seams(slots, count):
        row = lax.broadcasted_iota(jnp.int32, (SEAM, count), 0)
        return jnp.concatenate(
            [
                jnp.where(row < REACH, slots[index], slots[index + 1])
                for index in range(n_hours - 1)
            ]
            + [jnp.zeros((rest, count), jnp.float32)],
            axis=0,
        )

    seams = beside_seams([rims[index] for index in range(n_hours)], EDGE).T[:k]
    seams = jnp.concatenate([seams, jnp.zeros((k, EDGE - depth), jnp.float32)], axis=1)
    flat = [picks[index].astype(jnp.float32) for index in range(n_hours)]
    beside = beside_seams(
        [jnp.concatenate([pick[:SEAM], pick[SEAM:]], axis=1) for pick in flat], share
    )
    place = lane % SEAM
    crossing, weighted = [], []
    for side in (-1, 1):
        panel = jnp.zeros((k, EDGE), jnp.float32)
        for index in range(REACH):
            shift = side * (index + 1)
            from_place = place - shift
            inside = (from_place >= 0) & (from_place < SEAM)
            across = (place < REACH) != (from_place < REACH)
            mine = (lane >= depth * index) & (lane < depth * (index + 1))
            moved = pltpu.roll(seams, (depth * index + shift) % EDGE, 1)
            panel = jnp.where(inside & across & mine, moved, panel)
            step = REACH + shift
            weighted.append(taps[pl.ds(step, 1), pl.ds(starts[0], share)] * beside)
        crossing.append(panel)
    total += jnp.dot(
        jnp.concatenate(crossing, axis=1).astype(jnp.bfloat16),
        jnp.concatenate(weighted, axis=0).astype(jnp.bfloat16),
        preferred_element_type=jnp.float32,
    )
    bit = 1
    while bit < n_hours:
        copies[bit].wait_recv()
        arrived = near_in if bit == 1 else far_in
        total += arrived[bit - 1].astype(jnp.float32)
        bit *= 2
    local = total
    local_out[...] = local

    me = users * n_hours + hours
    folded, diagonal = pack(square(local))
    grams[me, pl.ds(0, k // 4), :] = folded
    grams[me, pl.ds(k // 4, 1), :] = diagonal
    pl.semaphore_wait(row_ready, n_users - 1)
    upper_half = users // (n_users // 2)
    outgoing, incoming = [], []
    for index in range(n_users):
        down = n_users - 2 - index
        down += (down - users + n_users) // n_users
        up = index + (index - users + n_users) // n_users
        target = upper_half * up + (1 - upper_half) * down if index < n_users - 1 else users
        for mask in range(n_hours - 1, -1, -1):
            if index == n_users - 1 and mask == 0:
                continue
            beside = flip(hours, mask)
            slot = target * n_hours + beside
            copy = pltpu.make_async_remote_copy(
                src_ref=grams.at[me],
                dst_ref=grams.at[me],
                send_sem=gram_send.at[slot],
                recv_sem=gram_recv.at[me],
                device_id={"users": target, "hours": beside},
                device_id_type=MESH,
            )
            copy.start()
            outgoing.append(copy)
            incoming.append(
                pltpu.make_async_remote_copy(
                    src_ref=grams.at[slot],
                    dst_ref=grams.at[slot],
                    send_sem=gram_send.at[slot],
                    recv_sem=gram_recv.at[slot],
                    device_id={"users": target, "hours": beside},
                    device_id_type=MESH,
                )
            )
    for copy in small + list(copies.values()):
        copy.wait_send()
    for copy in incoming:
        copy.wait_recv()
    gram = grams[0]
    for slot in range(1, n_users * n_hours):
        gram = gram + grams[slot]
    gram_out[...] = gram
    for copy in outgoing:
        copy.wait_send()


def finish(scale, local, gram, basis, triangle):
    upper, inverse = eliminate(unpack(gram[...]))
    triangle[...] = upper * scale
    high = inverse.astype(jnp.bfloat16)
    rest = (inverse - high.astype(jnp.float32)).astype(jnp.bfloat16)
    values = local[...]
    main = values.astype(jnp.bfloat16)
    minor = (values - main.astype(jnp.float32)).astype(jnp.bfloat16)
    basis[...] = jnp.dot(
        jnp.concatenate([high, rest, high], axis=1),
        jnp.concatenate([main, main, minor], axis=0),
        preferred_element_type=jnp.float32,
    )


def per_device(activity, cohort, tap_table, sketch):
    n_users, n_hours = lax.axis_size("users"), lax.axis_size("hours")
    rows, width = activity.shape
    k = sketch.shape[1]
    share = rows // n_hours
    dma = lambda count: pltpu.SemaphoreType.DMA((count,))
    vmem = pl.BlockSpec(memory_space=pltpu.VMEM)
    local, gram = pl.pallas_call(
        functools.partial(kernel, n_users, n_hours),
        out_shape=(
            pltpu.VMEM((k, share), jnp.float32),
            pltpu.VMEM((k // 4 + 1, 2 * k), jnp.float32),
        ),
        in_specs=[pl.BlockSpec(memory_space=pltpu.HBM)] * 4,
        out_specs=(vmem, vmem),
        scratch_shapes=[
            pltpu.VMEM((n_hours, share, width), jnp.bfloat16),
            pltpu.VMEM((1, rows), jnp.int32),
            pltpu.VMEM(tap_table.shape, jnp.float32),
            pltpu.VMEM((k, width), jnp.bfloat16),
            pltpu.VMEM((TAPS * k + PICK, width), jnp.bfloat16),
            pltpu.VMEM((TAPS, rows), jnp.float32),
            pltpu.VMEM((n_hours - 1, k, share), jnp.float32),
            pltpu.VMEM((n_hours - 1, k, share), jnp.float32),
            pltpu.VMEM((n_hours - 1, k, share), jnp.bfloat16),
            pltpu.VMEM((n_hours - 1, k, share), jnp.bfloat16),
            pltpu.VMEM((n_hours - 1, 2 * SEAM, share // 2), jnp.bfloat16),
            pltpu.VMEM((n_hours, 2 * SEAM, share // 2), jnp.bfloat16),
            pltpu.VMEM((n_hours, SEAM, EDGE), jnp.float32),
            pltpu.VMEM((n_users * n_hours, k // 4 + 1, 2 * k), jnp.float32),
            pltpu.SemaphoreType.REGULAR, dma(2 * n_hours), dma(3),
            dma(n_hours - 1), dma(n_hours - 1), dma(n_hours - 1), dma(n_hours - 1),
            dma(n_hours - 1), dma(n_hours - 1),
            dma(n_users * n_hours), dma(n_users * n_hours),
        ],
        compiler_params=pltpu.CompilerParams(
            collective_id=0, has_side_effects=True, vmem_limit_bytes=48 * 1024 * 1024
        ),
        name="range_finder",
    )(*(
        pltpu.with_memory_space_constraint(array, pltpu.HBM)
        for array in (activity, cohort[None, :], tap_table, sketch.T)
    ))
    basis, triangle = pl.pallas_call(
        functools.partial(finish, 1.0 / math.sqrt(rows * n_users)),
        out_shape=(
            jax.ShapeDtypeStruct((k, share), jnp.float32),
            jax.ShapeDtypeStruct((k, k), jnp.float32),
        ),
        in_specs=[vmem, vmem],
        out_specs=(vmem, vmem),
        compiler_params=pltpu.CompilerParams(vmem_limit_bytes=8 * 1024 * 1024),
        name="factor",
    )(
        pltpu.with_memory_space_constraint(local, pltpu.VMEM),
        pltpu.with_memory_space_constraint(gram, pltpu.VMEM),
    )
    return basis.T, triangle


def solution(mesh):
    return jax.shard_map(
        per_device,
        mesh=mesh,
        in_specs=(P(("groups", "users"), "hours"), P(("groups", "users")), P(), P("hours", None)),
        out_specs=(P(("groups", "users", "hours"), None), P("groups", None)),
        check_vma=False,
    )
```

```python
import functools
import math

import jax
import jax.numpy as jnp
from jax import lax
from jax.experimental import pallas as pl
from jax.experimental.pallas import tpu as pltpu
from jax.sharding import PartitionSpec as P

TAPS = 9
REACH = (TAPS - 1) // 2
EDGE = 128
SEAM = 2 * REACH
PICK = 16
PANEL = 16
HIGHEST = lax.Precision.HIGHEST
MESH = pl.DeviceIdType.MESH


def flip(index, mask):
    bit = 1
    while bit <= mask:
        if mask & bit:
            index = index + bit - 2 * bit * ((index // bit) % 2)
        bit *= 2
    return index


def dot_nt(a, b, precision=None):
    return lax.dot_general(
        a, b, (((1,), (1,)), ((), ())), precision=precision, preferred_element_type=jnp.float32
    )


def eliminate(gram):
    k = gram.shape[0]
    row_id = lax.broadcasted_iota(jnp.int32, (k, 2 * k), 0)
    lane_id = lax.broadcasted_iota(jnp.int32, (k, 2 * k), 1)
    eye = (row_id[:, :k] == lane_id[:, :k]).astype(jnp.float32)
    work = jnp.concatenate([gram, eye], axis=1)
    done = []
    for first in range(0, k, PANEL):
        rows = work.shape[0]
        below = lax.broadcasted_iota(jnp.int32, (rows, 2 * k), 0)
        cols = [
            jnp.broadcast_to(work[:, first + i : first + i + 1], (rows, 2 * k))
            for i in range(PANEL)
        ]
        for i in range(0, PANEL, 2):
            x, y = cols[i], cols[i + 1]
            a, b, d = x[i : i + 1, :], x[i + 1 : i + 2, :], y[i + 1 : i + 2, :]
            det = a * d - b * b
            inverse_det = 1.0 / det
            p = jnp.where(below > i + 1, d * x - b * y, 0.0) * inverse_det
            q = jnp.where(below > i + 1, a * y - b * x, 0.0) * inverse_det
            for later in range(i + 2, PANEL):
                cols[later] = cols[later] - (
                    p * x[later : later + 1, :] + q * y[later : later + 1, :]
                )
            top, second = work[i : i + 1, :], work[i + 1 : i + 2, :]
            work = work - (p * top + q * second)
            root = lax.rsqrt(a)
            done.append(top * root)
            done.append((second - (b * (1.0 / a)) * top) * (lax.rsqrt(det) * (a * root)))
        work = work[PANEL:]
    work = jnp.concatenate(done, axis=0)
    upper = jnp.where(row_id[:, :k] <= lane_id[:, :k], work[:, :k], 0.0)
    inverse = jnp.where(row_id[:, :k] >= lane_id[:, :k], work[:, k:], 0.0)
    return upper, inverse


def square(values):
    main = values.astype(jnp.bfloat16)
    minor = (values - main.astype(jnp.float32)).astype(jnp.bfloat16)
    return dot_nt(
        jnp.concatenate([main, main, minor], axis=1),
        jnp.concatenate([main, minor, main], axis=1),
    )


def pack(gram):
    k = gram.shape[0]
    half = k // 2
    row = lax.broadcasted_iota(jnp.int32, (half, half), 0)
    col = lax.broadcasted_iota(jnp.int32, (half, half), 1)
    corner = gram[half:, half:]
    folded = jnp.where(col >= row, gram[:half, :half], corner)
    wide = jnp.concatenate([folded, gram[:half, half:]], axis=1)
    diagonal = jnp.sum(jnp.where(row == col, corner, 0.0), axis=0, keepdims=True)
    diagonal = jnp.concatenate([diagonal, jnp.zeros((1, 2 * k - half), jnp.float32)], axis=1)
    quarter = half // 2
    return jnp.concatenate([wide[:quarter], wide[quarter:]], axis=1), diagonal


def unpack(packed):
    k = packed.shape[1] // 2
    half, quarter = k // 2, k // 4
    row = lax.broadcasted_iota(jnp.int32, (half, half), 0)
    col = lax.broadcasted_iota(jnp.int32, (half, half), 1)
    wide = jnp.concatenate([packed[:quarter, :k], packed[:quarter, k:]], axis=0)
    turned = wide.T
    upper, lower = wide[:, :half], turned[:half]
    corner = jnp.where(col < row, upper, lower)
    corner = jnp.where(col == row, packed[quarter : quarter + 1, :half], corner)
    first = jnp.where(col >= row, upper, lower)
    return jnp.concatenate(
        [
            jnp.concatenate([first, wide[:, half:]], axis=1),
            jnp.concatenate([turned[half:], corner], axis=1),
        ],
        axis=0,
    )


def combine(product, taps, k):
    total = taps[0:1, :] * product[:k]
    for step in range(1, TAPS):
        total += taps[step : step + 1, :] * product[step * k : (step + 1) * k]
    return total


def kernel(
    n_users, n_hours, activity, cohort_in, table_in, sketch_in, local_out, gram_out,
    block, cohort, table, sketch, shifted, taps, near_out, near_in, far_out, far_in,
    pick_out, picks, rims, grams,
    row_ready, load_sem, input_sem, part_send, part_recv, pick_send, pick_recv,
    rim_send, rim_recv, gram_send, gram_recv,
):
    users = lax.axis_index("users")
    hours = lax.axis_index("hours")
    rows, width = activity.shape
    k = sketch.shape[0]
    share = rows // n_hours
    half = share // 2

    order = list(range(n_hours - 1, 0, -1)) + [0]
    starts = [pl.multiple_of(flip(hours, mask) * share, share) for mask in range(n_hours)]
    inputs = [
        pltpu.make_async_copy(source, target, input_sem.at[i])
        for i, (source, target) in enumerate(
            ((cohort_in, cohort), (table_in, table), (sketch_in, sketch))
        )
    ]
    for copy in inputs:
        copy.start()
    loads = {}
    for mask in order:
        for part in range(2):
            load = pltpu.make_async_copy(
                activity.at[pl.ds(pl.multiple_of(starts[mask] + part * half, half), half), :],
                block.at[mask, pl.ds(part * half, half), :],
                load_sem.at[2 * mask + part],
            )
            loads[mask, part] = load

    def fetch(index):
        if index < n_hours:
            for part in range(2):
                loads[order[index], part].start()

    fetch(0)

    barrier = pltpu.get_barrier_semaphore()
    columns = [{"users": flip(users, far)} for far in range(n_users - 1, 0, -1)]
    for peer in [{"hours": flip(hours, mask)} for mask in range(n_hours - 1, 0, -1)] + columns:
        pl.semaphore_signal(barrier, inc=1, device_id=peer, device_id_type=MESH)

    pick_row = lax.broadcasted_iota(jnp.int32, (PICK, width), 0)
    pick_lane = lax.broadcasted_iota(jnp.int32, (PICK, width), 1)
    wanted = jnp.where(pick_row < REACH, width - REACH + pick_row, pick_row - REACH)
    shifted[pl.ds(TAPS * k, PICK), :] = (
        (pick_lane == wanted) & (pick_row < SEAM)
    ).astype(jnp.bfloat16)

    inputs[0].wait()
    inputs[1].wait()
    inputs[2].wait()
    fetch(1)
    middle = sketch[...].astype(jnp.float32)
    cohorts = table.shape[0]
    onehot = (
        lax.broadcasted_iota(jnp.int32, (cohorts, rows), 0) == cohort[...]
    ).astype(jnp.float32)
    taps[...] = lax.dot_general(
        table[...], onehot, (((0,), (0,)), ((), ())),
        precision=HIGHEST, preferred_element_type=jnp.float32,
    )

    lane = lax.broadcasted_iota(jnp.int32, (k, EDGE), 1)
    blank = jnp.zeros((k, EDGE), jnp.float32)
    padded = jnp.concatenate([blank, middle, blank], axis=1)
    for part in range(2):
        loads[order[0], part].wait()
    piece = width // 4
    products = [None, None]
    for first in range(0, width, piece):
        near_part = padded[:, first : first + piece + 2 * EDGE]
        for step in range(TAPS):
            shift = (step - REACH) % (piece + 2 * EDGE)
            moved = near_part if shift == 0 else pltpu.roll(near_part, shift, 1)
            shifted[pl.ds(step * k, k), pl.ds(first, piece)] = moved[
                :, EDGE : EDGE + piece
            ].astype(jnp.bfloat16)
        for part in range(2):
            partial = dot_nt(
                shifted[:, pl.ds(first, piece)],
                block[order[0], pl.ds(part * half, half), pl.ds(first, piece)],
            )
            products[part] = partial if first == 0 else products[part] + partial

    ends = jnp.where(
        lane < REACH,
        pltpu.roll(middle[:, width - EDGE :], REACH, 1),
        jnp.where(lane < SEAM, pltpu.roll(middle[:, :EDGE], REACH, 1), 0.0),
    )
    rims[hours] = jnp.concatenate(
        [ends.T[:SEAM], jnp.zeros((SEAM, EDGE - k), jnp.float32)], axis=1
    )

    small, copies = [], {}

    def send(source, target, send_sem, recv_sem, mask):
        copy = pltpu.make_async_remote_copy(
            src_ref=source, dst_ref=target, send_sem=send_sem, recv_sem=recv_sem,
            device_id={"hours": flip(hours, mask)}, device_id_type=MESH,
        )
        copy.start()
        return copy

    for index, mask in enumerate(order):
        if index:
            for part in range(2):
                loads[mask, part].wait()
        fetch(index + 2)
        sums, picked = [], []
        for part in range(2):
            if index:
                product = dot_nt(shifted[...], block[mask, pl.ds(part * half, half), :])
            else:
                product = products[part]
            start = pl.multiple_of(starts[mask] + part * half, half)
            sums.append(combine(product, taps[:, pl.ds(start, half)], k))
            picked.append(product[TAPS * k : TAPS * k + SEAM])
        total = jnp.concatenate(sums, axis=1)
        picked = jnp.concatenate(picked, axis=0).astype(jnp.bfloat16)
        if mask == order[0]:
            pl.semaphore_wait(barrier, n_hours + n_users - 2)
            for peer in columns:
                pl.semaphore_signal(row_ready, inc=1, device_id=peer, device_id_type=MESH)
            for other in range(1, n_hours):
                small.append(send(
                    rims.at[hours], rims.at[hours], rim_send.at[other - 1],
                    rim_recv.at[other - 1], other,
                ))
        if mask == 0:
            picks[hours] = picked
            continue
        bit = 1
        while mask + bit < n_hours and bit < mask & -mask:
            copies[mask + bit].wait()
            arrived = near_in if bit == 1 else far_in
            total += arrived[mask + bit - 1].astype(jnp.float32)
            bit *= 2
        near = mask % 2 == 1
        source, target = (near_out, near_in) if near else (far_out, far_in)
        source[mask - 1] = total.astype(source.dtype)
        copies[mask] = send(
            source.at[mask - 1], target.at[mask - 1], part_send.at[mask - 1],
            part_recv.at[mask - 1], mask & -mask,
        )
        pick_out[mask - 1] = picked
        small.append(send(
            pick_out.at[mask - 1], picks.at[hours], pick_send.at[mask - 1],
            pick_recv.at[mask - 1], mask,
        ))

    for copy in small:
        copy.wait()

    depth = EDGE // REACH
    rest = depth - SEAM * (n_hours - 1)

    def beside_seams(slots, count):
        row = lax.broadcasted_iota(jnp.int32, (SEAM, count), 0)
        return jnp.concatenate(
            [
                jnp.where(row < REACH, slots[index], slots[index + 1])
                for index in range(n_hours - 1)
            ]
            + [jnp.zeros((rest, count), jnp.float32)],
            axis=0,
        )

    seams = beside_seams([rims[index] for index in range(n_hours)], EDGE).T[:k]
    seams = jnp.concatenate([seams, jnp.zeros((k, EDGE - depth), jnp.float32)], axis=1)
    flat = [picks[index].astype(jnp.float32) for index in range(n_hours)]
    beside = beside_seams(
        [jnp.concatenate([pick[:SEAM], pick[SEAM:]], axis=1) for pick in flat], share
    )
    place = lane % SEAM
    crossing, weighted = [], []
    for side in (-1, 1):
        panel = jnp.zeros((k, EDGE), jnp.float32)
        for index in range(REACH):
            shift = side * (index + 1)
            from_place = place - shift
            inside = (from_place >= 0) & (from_place < SEAM)
            across = (place < REACH) != (from_place < REACH)
            mine = (lane >= depth * index) & (lane < depth * (index + 1))
            moved = pltpu.roll(seams, (depth * index + shift) % EDGE, 1)
            panel = jnp.where(inside & across & mine, moved, panel)
            step = REACH + shift
            weighted.append(taps[pl.ds(step, 1), pl.ds(starts[0], share)] * beside)
        crossing.append(panel)
    total += jnp.dot(
        jnp.concatenate(crossing, axis=1).astype(jnp.bfloat16),
        jnp.concatenate(weighted, axis=0).astype(jnp.bfloat16),
        preferred_element_type=jnp.float32,
    )
    bit = 1
    while bit < n_hours:
        copies[bit].wait()
        arrived = near_in if bit == 1 else far_in
        total += arrived[bit - 1].astype(jnp.float32)
        bit *= 2
    local = total
    local_out[...] = local

    me = users * n_hours + hours
    folded, diagonal = pack(square(local))
    grams[me, pl.ds(0, k // 4), :] = folded
    grams[me, pl.ds(k // 4, 1), :] = diagonal
    pl.semaphore_wait(row_ready, n_users - 1)
    upper_half = users // (n_users // 2)
    outgoing, incoming = [], []
    for index in range(n_users):
        down = n_users - 2 - index
        down += (down - users + n_users) // n_users
        up = index + (index - users + n_users) // n_users
        target = upper_half * up + (1 - upper_half) * down if index < n_users - 1 else users
        for mask in [code ^ 1 for code in range(n_hours - 1, -1, -1)]:
            if index == n_users - 1 and mask == 0:
                continue
            beside = flip(hours, mask)
            slot = target * n_hours + beside
            copy = pltpu.make_async_remote_copy(
                src_ref=grams.at[me],
                dst_ref=grams.at[me],
                send_sem=gram_send.at[slot],
                recv_sem=gram_recv.at[me],
                device_id={"users": target, "hours": beside},
                device_id_type=MESH,
            )
            copy.start()
            outgoing.append(copy)
            incoming.append(
                pltpu.make_async_remote_copy(
                    src_ref=grams.at[slot],
                    dst_ref=grams.at[slot],
                    send_sem=gram_send.at[slot],
                    recv_sem=gram_recv.at[slot],
                    device_id={"users": target, "hours": beside},
                    device_id_type=MESH,
                )
            )
    for copy in incoming:
        copy.wait_recv()
    gram = grams[0]
    for slot in range(1, n_users * n_hours):
        gram = gram + grams[slot]
    gram_out[...] = gram
    for copy in outgoing:
        copy.wait_send()


def finish(scale, local, gram, basis, triangle):
    upper, inverse = eliminate(unpack(gram[...]))
    triangle[...] = upper * scale
    high = inverse.astype(jnp.bfloat16)
    rest = (inverse - high.astype(jnp.float32)).astype(jnp.bfloat16)
    values = local[...]
    main = values.astype(jnp.bfloat16)
    minor = (values - main.astype(jnp.float32)).astype(jnp.bfloat16)
    basis[...] = jnp.dot(
        jnp.concatenate([high, rest, high], axis=1),
        jnp.concatenate([main, main, minor], axis=0),
        preferred_element_type=jnp.float32,
    )


def per_device(activity, cohort, tap_table, sketch):
    n_users, n_hours = lax.axis_size("users"), lax.axis_size("hours")
    rows, width = activity.shape
    k = sketch.shape[1]
    share = rows // n_hours
    dma = lambda count: pltpu.SemaphoreType.DMA((count,))
    vmem = pl.BlockSpec(memory_space=pltpu.VMEM)
    local, gram = pl.pallas_call(
        functools.partial(kernel, n_users, n_hours),
        out_shape=(
            pltpu.VMEM((k, share), jnp.float32),
            pltpu.VMEM((k // 4 + 1, 2 * k), jnp.float32),
        ),
        in_specs=[pl.BlockSpec(memory_space=pltpu.HBM)] * 4,
        out_specs=(vmem, vmem),
        scratch_shapes=[
            pltpu.VMEM((n_hours, share, width), jnp.bfloat16),
            pltpu.VMEM((1, rows), jnp.int32),
            pltpu.VMEM(tap_table.shape, jnp.float32),
            pltpu.VMEM((k, width), jnp.bfloat16),
            pltpu.VMEM((TAPS * k + PICK, width), jnp.bfloat16),
            pltpu.VMEM((TAPS, rows), jnp.float32),
            pltpu.VMEM((n_hours - 1, k, share), jnp.float32),
            pltpu.VMEM((n_hours - 1, k, share), jnp.float32),
            pltpu.VMEM((n_hours - 1, k, share), jnp.bfloat16),
            pltpu.VMEM((n_hours - 1, k, share), jnp.bfloat16),
            pltpu.VMEM((n_hours - 1, 2 * SEAM, share // 2), jnp.bfloat16),
            pltpu.VMEM((n_hours, 2 * SEAM, share // 2), jnp.bfloat16),
            pltpu.VMEM((n_hours, SEAM, EDGE), jnp.float32),
            pltpu.VMEM((n_users * n_hours, k // 4 + 1, 2 * k), jnp.float32),
            pltpu.SemaphoreType.REGULAR, dma(2 * n_hours), dma(3),
            dma(n_hours - 1), dma(n_hours - 1), dma(n_hours - 1), dma(n_hours - 1),
            dma(n_hours - 1), dma(n_hours - 1),
            dma(n_users * n_hours), dma(n_users * n_hours),
        ],
        compiler_params=pltpu.CompilerParams(
            collective_id=0, has_side_effects=True, vmem_limit_bytes=48 * 1024 * 1024
        ),
        name="range_finder",
    )(*(
        pltpu.with_memory_space_constraint(array, pltpu.HBM)
        for array in (activity, cohort[None, :], tap_table, sketch.T)
    ))
    basis, triangle = pl.pallas_call(
        functools.partial(finish, 1.0 / math.sqrt(rows * n_users)),
        out_shape=(
            jax.ShapeDtypeStruct((k, share), jnp.float32),
            jax.ShapeDtypeStruct((k, k), jnp.float32),
        ),
        in_specs=[vmem, vmem],
        out_specs=(vmem, vmem),
        compiler_params=pltpu.CompilerParams(vmem_limit_bytes=8 * 1024 * 1024),
        name="factor",
    )(
        pltpu.with_memory_space_constraint(local, pltpu.VMEM),
        pltpu.with_memory_space_constraint(gram, pltpu.VMEM),
    )
    return basis.T, triangle


def solution(mesh):
    return jax.shard_map(
        per_device,
        mesh=mesh,
        in_specs=(P(("groups", "users"), "hours"), P(("groups", "users")), P(), P("hours", None)),
        out_specs=(P(("groups", "users", "hours"), None), P("groups", None)),
        check_vma=False,
    )
```

```python
import functools
import math

import jax
import jax.numpy as jnp
from jax import lax
from jax.experimental import pallas as pl
from jax.experimental.pallas import tpu as pltpu
from jax.sharding import PartitionSpec as P

TAPS = 9
REACH = (TAPS - 1) // 2
EDGE = 128
SEAM = 2 * REACH
PICK = 16
PANEL = 16
HIGHEST = lax.Precision.HIGHEST
MESH = pl.DeviceIdType.MESH


def flip(index, mask):
    bit = 1
    while bit <= mask:
        if mask & bit:
            index = index + bit - 2 * bit * ((index // bit) % 2)
        bit *= 2
    return index


def dot_nt(a, b, precision=None):
    return lax.dot_general(
        a, b, (((1,), (1,)), ((), ())), precision=precision, preferred_element_type=jnp.float32
    )


def eliminate(gram):
    k = gram.shape[0]
    row_id = lax.broadcasted_iota(jnp.int32, (k, 2 * k), 0)
    lane_id = lax.broadcasted_iota(jnp.int32, (k, 2 * k), 1)
    eye = (row_id[:, :k] == lane_id[:, :k]).astype(jnp.float32)
    work = jnp.concatenate([gram, eye], axis=1)
    done = []
    for first in range(0, k, PANEL):
        rows = work.shape[0]
        below = lax.broadcasted_iota(jnp.int32, (rows, 2 * k), 0)
        cols = [
            jnp.broadcast_to(work[:, first + i : first + i + 1], (rows, 2 * k))
            for i in range(PANEL)
        ]
        for i in range(0, PANEL, 2):
            x, y = cols[i], cols[i + 1]
            a, b, d = x[i : i + 1, :], x[i + 1 : i + 2, :], y[i + 1 : i + 2, :]
            det = a * d - b * b
            inverse_det = 1.0 / det
            p = jnp.where(below > i + 1, d * x - b * y, 0.0) * inverse_det
            q = jnp.where(below > i + 1, a * y - b * x, 0.0) * inverse_det
            for later in range(i + 2, PANEL):
                cols[later] = cols[later] - (
                    p * x[later : later + 1, :] + q * y[later : later + 1, :]
                )
            top, second = work[i : i + 1, :], work[i + 1 : i + 2, :]
            work = work - (p * top + q * second)
            root = lax.rsqrt(a)
            done.append(top * root)
            done.append((second - (b * (1.0 / a)) * top) * (lax.rsqrt(det) * (a * root)))
        work = work[PANEL:]
    work = jnp.concatenate(done, axis=0)
    upper = jnp.where(row_id[:, :k] <= lane_id[:, :k], work[:, :k], 0.0)
    inverse = jnp.where(row_id[:, :k] >= lane_id[:, :k], work[:, k:], 0.0)
    return upper, inverse


def square(values):
    main = values.astype(jnp.bfloat16)
    minor = (values - main.astype(jnp.float32)).astype(jnp.bfloat16)
    return dot_nt(
        jnp.concatenate([main, main, minor], axis=1),
        jnp.concatenate([main, minor, main], axis=1),
    )


def pack(gram):
    k = gram.shape[0]
    half = k // 2
    row = lax.broadcasted_iota(jnp.int32, (half, half), 0)
    col = lax.broadcasted_iota(jnp.int32, (half, half), 1)
    corner = gram[half:, half:]
    folded = jnp.where(col >= row, gram[:half, :half], corner)
    wide = jnp.concatenate([folded, gram[:half, half:]], axis=1)
    diagonal = jnp.sum(jnp.where(row == col, corner, 0.0), axis=0, keepdims=True)
    diagonal = jnp.concatenate([diagonal, jnp.zeros((1, 2 * k - half), jnp.float32)], axis=1)
    quarter = half // 2
    return jnp.concatenate([wide[:quarter], wide[quarter:]], axis=1), diagonal


def unpack(packed):
    k = packed.shape[1] // 2
    half, quarter = k // 2, k // 4
    row = lax.broadcasted_iota(jnp.int32, (half, half), 0)
    col = lax.broadcasted_iota(jnp.int32, (half, half), 1)
    wide = jnp.concatenate([packed[:quarter, :k], packed[:quarter, k:]], axis=0)
    turned = wide.T
    upper, lower = wide[:, :half], turned[:half]
    corner = jnp.where(col < row, upper, lower)
    corner = jnp.where(col == row, packed[quarter : quarter + 1, :half], corner)
    first = jnp.where(col >= row, upper, lower)
    return jnp.concatenate(
        [
            jnp.concatenate([first, wide[:, half:]], axis=1),
            jnp.concatenate([turned[half:], corner], axis=1),
        ],
        axis=0,
    )


def combine(product, taps, k):
    total = taps[0:1, :] * product[:k]
    for step in range(1, TAPS):
        total += taps[step : step + 1, :] * product[step * k : (step + 1) * k]
    return total


def kernel(
    n_users, n_hours, activity, cohort_in, table_in, sketch_in, local_out, gram_out,
    block, cohort, table, sketch, shifted, taps, near_out, near_in, far_out, far_in,
    pick_out, picks, rims, grams,
    row_ready, load_sem, input_sem, part_send, part_recv, pick_send, pick_recv,
    rim_send, rim_recv, gram_send, gram_recv,
):
    users = lax.axis_index("users")
    hours = lax.axis_index("hours")
    rows, width = activity.shape
    k = sketch.shape[0]
    share = rows // n_hours
    half = share // 2

    order = list(range(n_hours - 1, 0, -1)) + [0]
    starts = [pl.multiple_of(flip(hours, mask) * share, share) for mask in range(n_hours)]
    inputs = [
        pltpu.make_async_copy(source, target, input_sem.at[i])
        for i, (source, target) in enumerate(
            ((cohort_in, cohort), (table_in, table), (sketch_in, sketch))
        )
    ]
    for copy in inputs:
        copy.start()
    loads = {}
    for mask in order:
        for part in range(2):
            load = pltpu.make_async_copy(
                activity.at[pl.ds(pl.multiple_of(starts[mask] + part * half, half), half), :],
                block.at[mask, pl.ds(part * half, half), :],
                load_sem.at[2 * mask + part],
            )
            loads[mask, part] = load

    def fetch(index):
        if index < n_hours:
            for part in range(2):
                loads[order[index], part].start()

    fetch(0)

    barrier = pltpu.get_barrier_semaphore()
    columns = [{"users": flip(users, far)} for far in range(n_users - 1, 0, -1)]
    for peer in [{"hours": flip(hours, mask)} for mask in range(n_hours - 1, 0, -1)] + columns:
        pl.semaphore_signal(barrier, inc=1, device_id=peer, device_id_type=MESH)

    pick_row = lax.broadcasted_iota(jnp.int32, (PICK, width), 0)
    pick_lane = lax.broadcasted_iota(jnp.int32, (PICK, width), 1)
    wanted = jnp.where(pick_row < REACH, width - REACH + pick_row, pick_row - REACH)
    shifted[pl.ds(TAPS * k, PICK), :] = (
        (pick_lane == wanted) & (pick_row < SEAM)
    ).astype(jnp.bfloat16)

    inputs[0].wait()
    inputs[1].wait()
    inputs[2].wait()
    fetch(1)
    middle = sketch[...].astype(jnp.float32)
    cohorts = table.shape[0]
    onehot = (
        lax.broadcasted_iota(jnp.int32, (cohorts, rows), 0) == cohort[...]
    ).astype(jnp.float32)
    taps[...] = lax.dot_general(
        table[...], onehot, (((0,), (0,)), ((), ())),
        precision=HIGHEST, preferred_element_type=jnp.float32,
    )

    lane = lax.broadcasted_iota(jnp.int32, (k, EDGE), 1)
    blank = jnp.zeros((k, EDGE), jnp.float32)
    padded = jnp.concatenate([blank, middle, blank], axis=1)
    for part in range(2):
        loads[order[0], part].wait()
    piece = width // 4
    products = [None, None]
    for first in range(0, width, piece):
        near_part = padded[:, first : first + piece + 2 * EDGE]
        for step in range(TAPS):
            shift = (step - REACH) % (piece + 2 * EDGE)
            moved = near_part if shift == 0 else pltpu.roll(near_part, shift, 1)
            shifted[pl.ds(step * k, k), pl.ds(first, piece)] = moved[
                :, EDGE : EDGE + piece
            ].astype(jnp.bfloat16)
        for part in range(2):
            partial = dot_nt(
                shifted[:, pl.ds(first, piece)],
                block[order[0], pl.ds(part * half, half), pl.ds(first, piece)],
            )
            products[part] = partial if first == 0 else products[part] + partial

    ends = jnp.where(
        lane < REACH,
        pltpu.roll(middle[:, width - EDGE :], REACH, 1),
        jnp.where(lane < SEAM, pltpu.roll(middle[:, :EDGE], REACH, 1), 0.0),
    )
    rims[hours] = jnp.concatenate(
        [ends.T[:SEAM], jnp.zeros((SEAM, EDGE - k), jnp.float32)], axis=1
    )

    small, copies = [], {}

    def send(source, target, send_sem, recv_sem, mask):
        copy = pltpu.make_async_remote_copy(
            src_ref=source, dst_ref=target, send_sem=send_sem, recv_sem=recv_sem,
            device_id={"hours": flip(hours, mask)}, device_id_type=MESH,
        )
        copy.start()
        return copy

    for index, mask in enumerate(order):
        if index:
            for part in range(2):
                loads[mask, part].wait()
        fetch(index + 2)
        sums, picked = [], []
        for part in range(2):
            if index:
                product = dot_nt(shifted[...], block[mask, pl.ds(part * half, half), :])
            else:
                product = products[part]
            start = pl.multiple_of(starts[mask] + part * half, half)
            sums.append(combine(product, taps[:, pl.ds(start, half)], k))
            picked.append(product[TAPS * k : TAPS * k + SEAM])
        total = jnp.concatenate(sums, axis=1)
        picked = jnp.concatenate(picked, axis=0).astype(jnp.bfloat16)
        if mask == order[0]:
            pl.semaphore_wait(barrier, n_hours + n_users - 2)
        if mask == 0:
            picks[hours] = picked
            continue
        bit = 1
        while mask + bit < n_hours and bit < mask & -mask:
            copies[mask + bit].wait_recv()
            arrived = near_in if bit == 1 else far_in
            total += arrived[mask + bit - 1].astype(jnp.float32)
            bit *= 2
        near = mask % 2 == 1
        source, target = (near_out, near_in) if near else (far_out, far_in)
        source[mask - 1] = total.astype(source.dtype)
        copies[mask] = send(
            source.at[mask - 1], target.at[mask - 1], part_send.at[mask - 1],
            part_recv.at[mask - 1], mask & -mask,
        )
        if mask == order[0]:
            for peer in columns:
                pl.semaphore_signal(row_ready, inc=1, device_id=peer, device_id_type=MESH)
            for other in range(1, n_hours):
                small.append(send(
                    rims.at[hours], rims.at[hours], rim_send.at[other - 1],
                    rim_recv.at[other - 1], other,
                ))
        pick_out[mask - 1] = picked
        small.append(send(
            pick_out.at[mask - 1], picks.at[hours], pick_send.at[mask - 1],
            pick_recv.at[mask - 1], mask,
        ))

    for copy in small:
        copy.wait_recv()

    depth = EDGE // REACH
    rest = depth - SEAM * (n_hours - 1)

    def beside_seams(slots, count):
        row = lax.broadcasted_iota(jnp.int32, (SEAM, count), 0)
        return jnp.concatenate(
            [
                jnp.where(row < REACH, slots[index], slots[index + 1])
                for index in range(n_hours - 1)
            ]
            + [jnp.zeros((rest, count), jnp.float32)],
            axis=0,
        )

    seams = beside_seams([rims[index] for index in range(n_hours)], EDGE).T[:k]
    seams = jnp.concatenate([seams, jnp.zeros((k, EDGE - depth), jnp.float32)], axis=1)
    flat = [picks[index].astype(jnp.float32) for index in range(n_hours)]
    beside = beside_seams(
        [jnp.concatenate([pick[:SEAM], pick[SEAM:]], axis=1) for pick in flat], share
    )
    place = lane % SEAM
    crossing, weighted = [], []
    for side in (-1, 1):
        panel = jnp.zeros((k, EDGE), jnp.float32)
        for index in range(REACH):
            shift = side * (index + 1)
            from_place = place - shift
            inside = (from_place >= 0) & (from_place < SEAM)
            across = (place < REACH) != (from_place < REACH)
            mine = (lane >= depth * index) & (lane < depth * (index + 1))
            moved = pltpu.roll(seams, (depth * index + shift) % EDGE, 1)
            panel = jnp.where(inside & across & mine, moved, panel)
            step = REACH + shift
            weighted.append(taps[pl.ds(step, 1), pl.ds(starts[0], share)] * beside)
        crossing.append(panel)
    total += jnp.dot(
        jnp.concatenate(crossing, axis=1).astype(jnp.bfloat16),
        jnp.concatenate(weighted, axis=0).astype(jnp.bfloat16),
        preferred_element_type=jnp.float32,
    )
    bit = 1
    while bit < n_hours:
        copies[bit].wait_recv()
        arrived = near_in if bit == 1 else far_in
        total += arrived[bit - 1].astype(jnp.float32)
        bit *= 2
    local = total
    local_out[...] = local

    me = users * n_hours + hours
    folded, diagonal = pack(square(local))
    grams[me, pl.ds(0, k // 4), :] = folded
    grams[me, pl.ds(k // 4, 1), :] = diagonal
    pl.semaphore_wait(row_ready, n_users - 1)
    upper_half = users // (n_users // 2)
    outgoing, incoming = [], []
    for index in range(n_users):
        down = n_users - 2 - index
        down += (down - users + n_users) // n_users
        up = index + (index - users + n_users) // n_users
        target = upper_half * up + (1 - upper_half) * down if index < n_users - 1 else users
        for mask in [code ^ 1 for code in range(n_hours - 1, -1, -1)]:
            if index == n_users - 1 and mask == 0:
                continue
            beside = flip(hours, mask)
            slot = target * n_hours + beside
            copy = pltpu.make_async_remote_copy(
                src_ref=grams.at[me],
                dst_ref=grams.at[me],
                send_sem=gram_send.at[slot],
                recv_sem=gram_recv.at[me],
                device_id={"users": target, "hours": beside},
                device_id_type=MESH,
            )
            copy.start()
            outgoing.append(copy)
            incoming.append(
                pltpu.make_async_remote_copy(
                    src_ref=grams.at[slot],
                    dst_ref=grams.at[slot],
                    send_sem=gram_send.at[slot],
                    recv_sem=gram_recv.at[slot],
                    device_id={"users": target, "hours": beside},
                    device_id_type=MESH,
                )
            )
    for copy in small + list(copies.values()):
        copy.wait_send()
    for copy in incoming:
        copy.wait_recv()
    gram = grams[0]
    for slot in range(1, n_users * n_hours):
        gram = gram + grams[slot]
    gram_out[...] = gram
    for copy in outgoing:
        copy.wait_send()


def finish(scale, local, gram, basis, triangle):
    upper, inverse = eliminate(unpack(gram[...]))
    triangle[...] = upper * scale
    high = inverse.astype(jnp.bfloat16)
    rest = (inverse - high.astype(jnp.float32)).astype(jnp.bfloat16)
    values = local[...]
    main = values.astype(jnp.bfloat16)
    minor = (values - main.astype(jnp.float32)).astype(jnp.bfloat16)
    basis[...] = jnp.dot(
        jnp.concatenate([high, rest, high], axis=1),
        jnp.concatenate([main, main, minor], axis=0),
        preferred_element_type=jnp.float32,
    )


def per_device(activity, cohort, tap_table, sketch):
    n_users, n_hours = lax.axis_size("users"), lax.axis_size("hours")
    rows, width = activity.shape
    k = sketch.shape[1]
    share = rows // n_hours
    dma = lambda count: pltpu.SemaphoreType.DMA((count,))
    vmem = pl.BlockSpec(memory_space=pltpu.VMEM)
    local, gram = pl.pallas_call(
        functools.partial(kernel, n_users, n_hours),
        out_shape=(
            pltpu.VMEM((k, share), jnp.float32),
            pltpu.VMEM((k // 4 + 1, 2 * k), jnp.float32),
        ),
        in_specs=[pl.BlockSpec(memory_space=pltpu.HBM)] * 4,
        out_specs=(vmem, vmem),
        scratch_shapes=[
            pltpu.VMEM((n_hours, share, width), jnp.bfloat16),
            pltpu.VMEM((1, rows), jnp.int32),
            pltpu.VMEM(tap_table.shape, jnp.float32),
            pltpu.VMEM((k, width), jnp.bfloat16),
            pltpu.VMEM((TAPS * k + PICK, width), jnp.bfloat16),
            pltpu.VMEM((TAPS, rows), jnp.float32),
            pltpu.VMEM((n_hours - 1, k, share), jnp.float32),
            pltpu.VMEM((n_hours - 1, k, share), jnp.float32),
            pltpu.VMEM((n_hours - 1, k, share), jnp.bfloat16),
            pltpu.VMEM((n_hours - 1, k, share), jnp.bfloat16),
            pltpu.VMEM((n_hours - 1, 2 * SEAM, share // 2), jnp.bfloat16),
            pltpu.VMEM((n_hours, 2 * SEAM, share // 2), jnp.bfloat16),
            pltpu.VMEM((n_hours, SEAM, EDGE), jnp.float32),
            pltpu.VMEM((n_users * n_hours, k // 4 + 1, 2 * k), jnp.float32),
            pltpu.SemaphoreType.REGULAR, dma(2 * n_hours), dma(3),
            dma(n_hours - 1), dma(n_hours - 1), dma(n_hours - 1), dma(n_hours - 1),
            dma(n_hours - 1), dma(n_hours - 1),
            dma(n_users * n_hours), dma(n_users * n_hours),
        ],
        compiler_params=pltpu.CompilerParams(
            collective_id=0, has_side_effects=True, vmem_limit_bytes=48 * 1024 * 1024
        ),
        name="range_finder",
    )(*(
        pltpu.with_memory_space_constraint(array, pltpu.HBM)
        for array in (activity, cohort[None, :], tap_table, sketch.T)
    ))
    basis, triangle = pl.pallas_call(
        functools.partial(finish, 1.0 / math.sqrt(rows * n_users)),
        out_shape=(
            jax.ShapeDtypeStruct((k, share), jnp.float32),
            jax.ShapeDtypeStruct((k, k), jnp.float32),
        ),
        in_specs=[vmem, vmem],
        out_specs=(vmem, vmem),
        compiler_params=pltpu.CompilerParams(vmem_limit_bytes=8 * 1024 * 1024),
        name="factor",
    )(
        pltpu.with_memory_space_constraint(local, pltpu.VMEM),
        pltpu.with_memory_space_constraint(gram, pltpu.VMEM),
    )
    return basis.T, triangle


def solution(mesh):
    return jax.shard_map(
        per_device,
        mesh=mesh,
        in_specs=(P(("groups", "users"), "hours"), P(("groups", "users")), P(), P("hours", None)),
        out_specs=(P(("groups", "users", "hours"), None), P("groups", None)),
        check_vma=False,
    )
```
